32 devices in a mesh: row: 4 (over z), col: 8 (over y, x, core).
Axes of the slice: x: 2, y: 2, z: 4, core: 2. Of those that a mesh axis runs over, the one named last changes fastest.
Arguments:
- right_side: float32 [4096, 4, 128], P(('row', 'col')), may hold values from -60 to 60
- cluster_of: int32 [4096], P(('row', 'col')), may hold values from 0 to 4095, as said below
- near_rows: int32 [12288], P(('row', 'col')), may hold values from 0 to 127
- near_columns: int32 [12288], P(('row', 'col')), may hold values from 0 to 191, as said below
- near_blocks: bfloat16 [12288, 128, 128], P(('row', 'col')), may hold values from -1 to 1
- far_rows: int32 [32768], P(('row', 'col')), may hold values from 0 to 1023, as said below
- far_columns: int32 [32768], P(('row', 'col')), may hold values from 0 to 511
- far_rank: int32 [32768], P(('row', 'col')), may hold values from 4 to 16
- far_left: bfloat16 [32768, 16, 128], P(('row', 'col')), may hold values from -1.5 to 1.5
- far_right: bfloat16 [32768, 16, 128], P(('row', 'col')), may hold values from -0.5 to 0.5
Outputs:
- second_basis: float32 [4096, 4, 128], P(('row', 'col'))
- next_vector: float32 [4096, 4, 128], P(('row', 'col'))
- hessenberg: float32 [5, 4], replicated
The draws below stay inside these ranges and needn't reach their ends.
Inputs may be any that keep to these rules, and one draw needn't show every extreme that they name: `cluster_of`: A permutation of the cluster positions; position g belongs to the device of index g // 128 along row+col. Each device's blocks go to at most 8 blocks a destination device, and exactly 8 to some. `near_columns`: position 32 is the device's own first block; entries never point before the first or after the last block of cluster order. `far_rows`: in each device's list, the k-th group of 128 entries has rows in blocks k * 128 to (k + 1) * 128 - 1 of the row cluster.
All inputs are finite; a program needn't handle non-finite values.
Results may differ from the reference program's by a relative error of at most 0.0018.
The reference program's roundings to bfloat16 on the way (of `clustered` and `coefficients`) count: a program that leaves them out, or rounds other values in their place, can miss the bound.
Values may be sent and summed in bfloat16 or wider, within the bound.
A program may use at most 128 MiB of HBM per device.

```python
import math
import jax
import jax.numpy as jnp
from jax import lax

BLOCK_SIZE = 128
MAX_RANK = 16
SIDES = 4
BLOCKS_DEV = 128
NEAR_DEV = 384
FAR_DEV = 1024
BLOCKS = 4096
PANELS = 524288
CAPACITY = 8
HALO_BLOCKS = 32
ROW_CLUSTER = 1024
COL_CLUSTER = 512
FAR_GROUP = 128
N_COL = 8
DEVICES = 32


def draw_right_side(key, part):
    key_base, key_block, key_side = jax.random.split(key, 3)
    index = jnp.arange(BLOCKS, dtype=jnp.float32)
    rising = 0.5 + index / BLOCKS
    block_scale = jnp.exp(jax.random.uniform(key_block, (BLOCKS,), jnp.float32, math.log(0.6), math.log(2.4)))
    side_scale = jnp.exp(jax.random.uniform(key_side, (SIDES,), jnp.float32, math.log(0.3), math.log(3.0)))
    values = jnp.clip(jax.random.normal(key_base, (BLOCKS, SIDES, BLOCK_SIZE), jnp.float32), -3.0, 3.0)
    return values * (rising * block_scale)[:, None, None] * side_scale[None, :, None]


def draw_cluster_of(key, part):
    key_shift, key_source, key_target = jax.random.split(jax.random.fold_in(key, 7), 3)
    shifts = jax.random.permutation(key_shift, DEVICES).astype(jnp.int32)

    def one_order(single_key):
        return jax.random.permutation(single_key, BLOCKS_DEV).astype(jnp.int32)
    source_order = jax.vmap(one_order)(jax.random.split(key_source, DEVICES))
    target_order = jax.vmap(one_order)(jax.random.split(key_target, DEVICES))
    heavy = DEVICES // 4 * CAPACITY
    group = jnp.where(source_order < heavy, source_order // CAPACITY, DEVICES // 4 + (source_order - heavy) // (CAPACITY // 2))
    source = jnp.arange(DEVICES, dtype=jnp.int32)[:, None]
    target = (source + shifts[group]) % DEVICES
    position = target * BLOCKS_DEV + target_order[target, source_order]
    return position.reshape(-1).astype(jnp.int32)


def near_pairs(key):
    key_rows, key_offsets = jax.random.split(jax.random.fold_in(key, 11), 2)
    rows = jax.random.randint(key_rows, (DEVICES, NEAR_DEV), 0, BLOCKS_DEV).astype(jnp.int32)
    offsets = jax.random.randint(key_offsets, (DEVICES, NEAR_DEV), -HALO_BLOCKS, HALO_BLOCKS + 1).astype(jnp.int32)
    entry = jnp.arange(NEAR_DEV, dtype=jnp.int32)
    self_entry = (entry % 3 == 2) & ((entry - 2) // 3 < BLOCKS_DEV)
    rows = jnp.where(self_entry[None, :], ((entry - 2) // 3)[None, :], rows).astype(jnp.int32)
    offsets = jnp.where(self_entry[None, :], 0, offsets).astype(jnp.int32)
    rows = rows.at[:, 0].set(BLOCKS_DEV - 1).at[:, 1].set(0)
    offsets = offsets.at[:, 0].set(HALO_BLOCKS).at[:, 1].set(-HALO_BLOCKS)
    relative = rows + offsets
    device = jnp.arange(DEVICES, dtype=jnp.int32)[:, None]
    relative = jnp.where((device == 0) & (relative < 0), -relative - 1, relative)
    relative = jnp.where((device == DEVICES - 1) & (relative >= BLOCKS_DEV), 2 * BLOCKS_DEV - 1 - relative, relative)
    return (rows.reshape(-1), (relative + HALO_BLOCKS).reshape(-1).astype(jnp.int32))


def draw_near_rows(key, part):
    return near_pairs(key)[0]


def draw_near_columns(key, part):
    return near_pairs(key)[1]


def draw_near_blocks(key, part):
    key_noise, key_level, key_entry = jax.random.split(jax.random.fold_in(key, 17), 3)
    sigma = 1.0 / math.sqrt(BLOCK_SIZE)
    shape = (DEVICES * NEAR_DEV, BLOCK_SIZE, BLOCK_SIZE)
    noise = jax.random.normal(key_noise, shape, jnp.float32) * sigma
    noise = jnp.clip(noise, -0.35, 0.35)
    level = jnp.exp(jax.random.uniform(key_level, (DEVICES,), jnp.float32, math.log(0.15), math.log(0.5)))
    factor = jax.random.uniform(key_entry, (DEVICES, NEAR_DEV), jnp.float32, 0.7, 1.3)
    diagonal = (level[:, None] * factor).reshape(-1)
    identity = jnp.eye(BLOCK_SIZE, dtype=jnp.float32)
    return (noise + diagonal[:, None, None] * identity[None, :, :]).astype(jnp.bfloat16)


def draw_far_rows(key, part):
    offsets = jax.random.randint(jax.random.fold_in(key, 13), (DEVICES, FAR_DEV), 0, BLOCKS_DEV).astype(jnp.int32)
    offsets = offsets.at[:, 0].set(0).at[:, FAR_DEV - 1].set(BLOCKS_DEV - 1)
    bucket = jnp.arange(FAR_DEV, dtype=jnp.int32) // FAR_GROUP
    return (bucket[None, :] * BLOCKS_DEV + offsets).reshape(-1).astype(jnp.int32)


def set_ends(result, own_key, low, top_value):
    longest = result.shape.index(max(result.shape))
    spots = []
    for shift in (0, 1):
        where = [jax.random.randint(jax.random.fold_in(own_key, axis), (), 0, length) for axis, length in enumerate(result.shape)]
        where[longest] = (where[longest] + shift) % result.shape[longest]
        spots.append(tuple(where))
    return result.at[spots[0]].set(low).at[spots[1]].set(top_value)


def shard_levels(key, dims, shards, smallest, largest):
    level = 1.0
    for dim, shards_of in shards:
        draws = jax.random.uniform(jax.random.fold_in(jax.random.fold_in(key, 6), dim), (shards_of,), jnp.float32, smallest / len(shards), largest / len(shards))
        level = level * jnp.repeat(jnp.exp(draws), dims[dim] // shards_of).reshape((-1,) + (1,) * (len(dims) - 1 - dim))
    return level


def normal_values(key, shape, spread, reach, shards=(), kind=jnp.bfloat16):
    result = jax.random.normal(key, shape, jnp.float32) * spread
    if len(shards) > 0:
        result = shard_levels(key, shape, shards, -0.22, 0.18) * result
    return jnp.clip(result, min=-reach, max=reach).astype(kind)


def setup_inputs(seed: int = 0) -> dict:
    arg_keys = jax.random.split(jax.random.key(seed), 11)
    right_side = draw_right_side(jax.random.fold_in(arg_keys[10], 71), 0)
    cluster_of = draw_cluster_of(jax.random.fold_in(arg_keys[10], 71), 0)
    near_rows = draw_near_rows(jax.random.fold_in(arg_keys[10], 71), 0)
    near_columns = draw_near_columns(jax.random.fold_in(arg_keys[10], 71), 0)
    near_blocks = draw_near_blocks(jax.random.fold_in(arg_keys[10], 71), 0)
    far_rows = draw_far_rows(jax.random.fold_in(arg_keys[10], 71), 0)
    far_columns = set_ends(jax.random.randint(arg_keys[6], (DEVICES * FAR_DEV,), 0, COL_CLUSTER), jax.random.fold_in(arg_keys[6], 1), 0, COL_CLUSTER - 1).astype(jnp.int32)
    far_rank = set_ends(jax.random.randint(arg_keys[7], (DEVICES * FAR_DEV,), 4, MAX_RANK + 1), jax.random.fold_in(arg_keys[7], 1), 4, MAX_RANK).astype(jnp.int32)
    far_left = normal_values(arg_keys[8], (DEVICES * FAR_DEV, MAX_RANK, BLOCK_SIZE), MAX_RANK ** -0.5, 1.5, ((0, 32),))
    far_right = normal_values(arg_keys[9], (DEVICES * FAR_DEV, MAX_RANK, BLOCK_SIZE), BLOCK_SIZE ** -0.5, 0.5, ((0, 32),))
    return {"right_side": right_side, "cluster_of": cluster_of, "near_rows": near_rows, "near_columns": near_columns, "near_blocks": near_blocks, "far_rows": far_rows, "far_columns": far_columns, "far_rank": far_rank, "far_left": far_left, "far_right": far_right}


epsilon = 1e-06

def apply_operator(vector, cluster_of, near_rows, near_columns, near_blocks, far_rows, far_columns, far_rank, far_left, far_right):
    rounded = lax.optimization_barrier(vector.astype(jnp.bfloat16))
    clustered = jnp.zeros_like(rounded).at[cluster_of].set(rounded)
    padded = jnp.pad(clustered, ((HALO_BLOCKS, HALO_BLOCKS), (0, 0), (0, 0)))
    start_image = 0.5 * clustered.astype(jnp.float32)
    rank_index = jnp.arange(MAX_RANK, dtype=jnp.int32)

    def device_terms(image_sum, scanned):
        device, row_near, column_near, matrix_near, row_far, column_far, ranks_far, left_factor, right_factor = scanned
        offset = device * BLOCKS_DEV
        picked = padded[offset + column_near].astype(jnp.float32)
        near_out = jnp.einsum('ekp,eqp->eqk', matrix_near.astype(jnp.float32), picked, precision=lax.Precision.HIGHEST)
        image_sum = image_sum.at[offset + row_near].add(near_out)
        row_index = device // N_COL
        column_index = device % N_COL
        global_columns = (column_far // BLOCKS_DEV * N_COL + column_index) * BLOCKS_DEV + column_far % BLOCKS_DEV
        far_picked = clustered[global_columns].astype(jnp.float32)
        coefficients = jnp.einsum('etp,eqp->etq', right_factor.astype(jnp.float32), far_picked, precision=lax.Precision.HIGHEST)
        rank_mask = (rank_index[None, :] < ranks_far[:, None]).astype(jnp.float32)
        coefficients = lax.optimization_barrier((coefficients * rank_mask[:, :, None]).astype(jnp.bfloat16))
        far_out = jnp.einsum('etq,etk->eqk', coefficients.astype(jnp.float32), left_factor.astype(jnp.float32), precision=lax.Precision.HIGHEST)
        image_sum = image_sum.at[row_index * ROW_CLUSTER + row_far].add(far_out)
        return (image_sum, None)
    scanned = (jnp.arange(DEVICES, dtype=jnp.int32), near_rows.reshape(DEVICES, NEAR_DEV), near_columns.reshape(DEVICES, NEAR_DEV), near_blocks.reshape(DEVICES, NEAR_DEV, BLOCK_SIZE, BLOCK_SIZE), far_rows.reshape(DEVICES, FAR_DEV), far_columns.reshape(DEVICES, FAR_DEV), far_rank.reshape(DEVICES, FAR_DEV), far_left.reshape(DEVICES, FAR_DEV, MAX_RANK, BLOCK_SIZE), far_right.reshape(DEVICES, FAR_DEV, MAX_RANK, BLOCK_SIZE))
    image_sum, unused = lax.scan(device_terms, start_image, scanned)
    return image_sum[cluster_of]

def inner_mean(left_vector, right_vector):
    return lax.optimization_barrier(jnp.sum(left_vector * right_vector, axis=(0, 2))) / PANELS

def reference(right_side, cluster_of, near_rows, near_columns, near_blocks, far_rows, far_columns, far_rank, far_left, far_right):

    def operate(vector):
        return apply_operator(vector, cluster_of, near_rows, near_columns, near_blocks, far_rows, far_columns, far_rank, far_left, far_right)
    side_norm = jnp.sqrt(inner_mean(right_side, right_side) + epsilon)
    first = right_side / side_norm[None, :, None]
    image_one = operate(first)
    project_one = inner_mean(first, image_one)
    remainder = image_one - project_one[None, :, None] * first
    norm_two = jnp.sqrt(inner_mean(remainder, remainder) + epsilon)
    second_basis = remainder / norm_two[None, :, None]
    image_two = operate(second_basis)
    project_two = inner_mean(first, image_two)
    project_three = inner_mean(second_basis, image_two)
    next_vector = image_two - project_two[None, :, None] * first - project_three[None, :, None] * second_basis
    hessenberg = jnp.stack([side_norm, project_one, norm_two, project_two, project_three])
    return (second_basis, next_vector, hessenberg)
```

```python
import functools

import jax
import jax.numpy as jnp
from jax import lax
from jax.experimental import pallas as pl
from jax.experimental.pallas import tpu as pltpu
from jax.sharding import PartitionSpec as P

epsilon = 1e-06
MESH = pl.DeviceIdType.MESH
VMEM = pl.BlockSpec(memory_space=pltpu.VMEM)
LANES = 128
LIMIT = 56 * 2**20
TILE = 8
TOP = 32767.0


def coordinates(index, column_count):
    return (lax.div(index, column_count), lax.rem(index, column_count))


def enter(me, rows, columns):
    count = rows * columns
    barrier = pltpu.get_barrier_semaphore()

    @pl.loop(1, count)
    def _(k):
        pl.semaphore_signal(
            barrier,
            inc=1,
            device_id=coordinates(lax.rem(me + k, count), columns),
            device_id_type=MESH,
        )

    pl.semaphore_wait(barrier, count - 1)


def split_dot(picker, value, terms=3):
    total = None
    for _ in range(terms):
        part = value.astype(jnp.bfloat16)
        value = value - part.astype(jnp.float32)
        product = jnp.dot(picker, part, preferred_element_type=jnp.float32)
        total = product if total is None else total + product
    return total


def one_hot(condition):
    return jnp.where(condition, 1.0, 0.0).astype(jnp.bfloat16)


def remote(source, destination, sends, recvs, k, device):
    return pltpu.make_async_remote_copy(
        src_ref=source,
        dst_ref=destination,
        send_sem=sends.at[k],
        recv_sem=recvs.at[k],
        device_id=device,
        device_id_type=MESH,
    )


def near_group(sides, g, tables_ref, extended, near_ref, near_out, image):
    near_count = near_ref.shape[1]
    reach = extended.shape[0]
    blocks = image.shape[0]
    table = tables_ref[g]
    turned = table.T
    column = turned[:near_count, 0:1]
    pick = one_hot(
        column == lax.broadcasted_iota(jnp.int32, (near_count, reach), 1).astype(jnp.float32)
    )
    picked = jnp.dot(pick, extended[...], preferred_element_type=jnp.float32)
    batch = 8
    row_id = lax.rem(lax.broadcasted_iota(jnp.int32, (sides * batch, LANES), 0), batch)
    for j in range(near_count // batch):
        here = slice(j * batch, (j + 1) * batch)
        stacked = jnp.concatenate(
            [picked[here, s * LANES : (s + 1) * LANES] for s in range(sides)], axis=0
        ).astype(jnp.bfloat16)
        product = lax.dot_general(
            stacked,
            near_ref[g, here].reshape(batch * LANES, LANES),
            (((1,), (1,)), ((), ())),
            preferred_element_type=jnp.float32,
        )
        value = jnp.zeros((sides * batch, LANES), jnp.float32)
        for e in range(batch):
            value = jnp.where(row_id == e, product[:, e * LANES : (e + 1) * LANES], value)
        for s in range(sides):
            near_out[here, s * LANES : (s + 1) * LANES] = value[s * batch : (s + 1) * batch]
    place = one_hot(
        table[1:2, :near_count]
        == lax.broadcasted_iota(jnp.int32, (blocks, near_count), 0).astype(jnp.float32)
    )
    image[...] += split_dot(place, near_out[...])


def far_group(sides, g, tables_ref, everything, far_left, far_right, far_out):
    rows, blocks, width = everything.shape
    far_count, rank = far_left.shape[1:3]
    table = tables_ref[g]
    turned = table.T
    lanes = lax.broadcasted_iota(jnp.int32, (far_count, rows * blocks), 1).astype(jnp.float32)
    pick = one_hot(turned[:far_count, 0:1] == lanes)
    picked = jnp.dot(
        pick, everything[...].reshape(rows * blocks, width), preferred_element_type=jnp.float32
    )
    batch = 32
    shape = (sides * batch, batch * rank)
    entry = lax.rem(lax.broadcasted_iota(jnp.int32, shape, 0), batch)
    lane = lax.broadcasted_iota(jnp.int32, shape, 1)
    term = lax.rem(lane, rank).astype(jnp.float32)
    own_entry = lax.div(lane, rank) == entry
    for j in range(far_count // batch):
        here = slice(j * batch, (j + 1) * batch)
        stacked = jnp.concatenate(
            [picked[here, s * LANES : (s + 1) * LANES] for s in range(sides)], axis=0
        ).astype(jnp.bfloat16)
        product = lax.dot_general(
            stacked,
            far_right[g, here].reshape(batch * rank, LANES),
            (((1,), (1,)), ((), ())),
            preferred_element_type=jnp.float32,
        )
        ranks = jnp.concatenate([turned[here, 2:3]] * sides, axis=0)
        coefficients = jnp.where(own_entry & (term < ranks), product, 0.0).astype(jnp.bfloat16)
        value = jnp.dot(
            coefficients,
            far_left[g, here].reshape(batch * rank, LANES),
            preferred_element_type=jnp.float32,
        )
        for s in range(sides):
            far_out[here, s * LANES : (s + 1) * LANES] = value[s * batch : (s + 1) * batch]
    place = one_hot(
        table[1:2, :far_count]
        == lax.broadcasted_iota(jnp.int32, (blocks, far_count), 0).astype(jnp.float32)
    )
    return split_dot(place, far_out[...])


def iota(shape, dimension):
    return lax.broadcasted_iota(jnp.int32, shape, dimension)


def encode(value, scale):
    code = jnp.floor(jnp.clip(value * (TOP / scale), -TOP, TOP) + 0.5)
    return code.astype(jnp.int32).astype(jnp.int16)


def decode(code):
    return code.astype(jnp.int32).astype(jnp.float32)


def largest(value):
    top = jnp.max(jnp.abs(value), axis=0, keepdims=True)
    return jnp.maximum(jnp.max(top, axis=1, keepdims=True), 1e-30)


def total_of(value):
    return jnp.sum(jnp.sum(value, axis=0, keepdims=True), axis=1, keepdims=True)


def arnoldi_kernel(
    rows,
    columns,
    side_ref,
    cluster_ref,
    near_columns_ref,
    near_rows_ref,
    far_columns_ref,
    far_rows_ref,
    far_rank_ref,
    near_hbm,
    far_left_hbm,
    far_right_hbm,
    basis_ref,
    next_ref,
    entries_ref,
    near_tables,
    far_tables,
    sent,
    landed,
    sent_basis,
    landed_basis,
    sent_image,
    landed_image,
    first_ref,
    near_ref,
    far_left,
    far_right,
    own,
    basis,
    image,
    everything,
    extended,
    left,
    right,
    near_out,
    far_out,
    to_partner,
    from_partner,
    to_chips,
    from_chips,
    code_to,
    code_from,
    scale_to,
    scale_from,
    mine,
    parts,
    load_sem,
    halo_send,
    halo_recv,
    spread_send,
    spread_recv,
    pair_send,
    pair_recv,
    chip_send,
    chip_recv,
    scale_send,
    scale_recv,
    all_send,
    all_recv,
):
    row, column = lax.axis_index("row"), lax.axis_index("col")
    count = rows * columns
    me = row * columns + column
    blocks, width = first_ref.shape
    sides = width // LANES
    halo = left.shape[0]
    groups = far_left.shape[0]
    near_groups = near_ref.shape[0]
    pairs = columns // 2
    chip, core = lax.div(column, 2), lax.rem(column, 2)
    partner = 2 * chip + 1 - core
    panels = count * blocks * LANES
    lanes = [slice(s * LANES, (s + 1) * LANES) for s in range(sides)]
    capacity = (sent.shape[1] - TILE) // sides
    slots = count * capacity
    lane_row = iota((1, LANES), 1)

    def load(kind, g):
        source, target = (
            (near_hbm, near_ref),
            (far_left_hbm, far_left),
            (far_right_hbm, far_right),
        )[kind]
        return pltpu.make_async_copy(source.at[g], target.at[g], load_sem.at[kind, g])

    for kind, many in enumerate((near_groups, groups, groups)):

        @pl.loop(0, many)
        def _(g, kind=kind):
            load(kind, g).start()

    def to_all(n, source, destination, part):
        def copy(peer, there, here):
            return pltpu.make_async_remote_copy(
                src_ref=source.at[there, part],
                dst_ref=destination.at[here, part],
                send_sem=all_send.at[n],
                recv_sem=all_recv.at[n],
                device_id=coordinates(peer, columns),
                device_id_type=MESH,
            )

        def start():
            @pl.loop(1, count)
            def _(k):
                peer = lax.rem(me + k, count)
                copy(peer, peer, me).start()

            destination[me] = source[me]

        every = copy(lax.rem(me + 1, count), pl.ds(0, count - 1), pl.ds(0, count - 1))
        return start, every.wait_recv, every.wait_send

    def share(n, values):
        row_of = jnp.zeros((1, LANES), jnp.float32)
        for place, value in enumerate(values):
            row_of = row_of + jnp.where(lane_row == place, value, 0.0)
        mine[n] = jnp.broadcast_to(row_of, (TILE, LANES))

        def copy(peer, here):
            return pltpu.make_async_remote_copy(
                src_ref=mine.at[n] if here is not None else parts.at[n, pl.ds(0, count - 1)],
                dst_ref=parts.at[n, here if here is not None else pl.ds(0, count - 1)],
                send_sem=all_send.at[3 + n],
                recv_sem=all_recv.at[3 + n],
                device_id=coordinates(peer, columns),
                device_id_type=MESH,
            )

        @pl.loop(1, count)
        def _(k):
            copy(lax.rem(me + k, count), me).start()

        parts[n, me] = mine[n]
        every = copy(lax.rem(me + 1, count), None)

        def wait():
            every.wait_recv()
            every.wait_send()
            return parts[n, :, 0, :]

        return wait

    def single(total, place):
        return jnp.sum(jnp.where(lane_row == place, total, 0.0), axis=1, keepdims=True)

    cluster = cluster_ref[...]
    target = lax.div(cluster, blocks)
    turned = jnp.broadcast_to(cluster.astype(jnp.float32), (blocks, blocks)).T.astype(jnp.int32)
    turned_target = lax.div(turned, blocks)
    place = turned - turned_target * blocks
    square = (blocks, blocks)
    same = turned_target == target
    ranks = jnp.where(same & (iota(square, 1) < iota(square, 0)), 1, 0)
    rank_column = jnp.sum(ranks, axis=1, keepdims=True)
    ranks = jnp.where(same & (iota(square, 0) < iota(square, 1)), 1, 0)
    rank_row = jnp.sum(ranks, axis=0, keepdims=True)
    slot_shape = (slots, blocks)
    to_slot = one_hot(iota(slot_shape, 0) == target * capacity + rank_row)
    to_device = one_hot(lax.div(iota(slot_shape, 0), capacity) == target)
    marks = jnp.where(iota(square, 1) == rank_column, place + 1, 0)
    extra = jnp.dot(
        to_device,
        marks.astype(jnp.float32).astype(jnp.bfloat16),
        preferred_element_type=jnp.float32,
    )
    stride = [pl.ds(s, blocks, stride=sides) for s in range(sides)]
    for s in range(sides):
        value = side_ref[stride[s], :]
        extra = extra + jnp.where(lane_row == capacity + s, total_of(value * value), 0.0)
        picked = split_dot(to_slot, value)
        sent[:, s * capacity : (s + 1) * capacity, :] = picked.reshape(count, capacity, LANES)
    top = sides * capacity
    if capacity == TILE:
        sent[:, top:, :] = extra.reshape(count, TILE, LANES)
    else:
        sent[:, top:, :] = extra.reshape(count, capacity, LANES)[:, :TILE]
    enter(me, rows, columns)
    out_start, out_recv, out_send = to_all(0, sent, landed, pl.ds(0, top + TILE))
    out_start()

    near_tables[...] = jnp.zeros(near_tables.shape, jnp.float32)
    for g in range(near_groups):
        for spot, source in enumerate((near_columns_ref, near_rows_ref)):
            near_tables[g, spot : spot + 1] = source[g : g + 1].astype(jnp.float32)
    far_tables[...] = jnp.zeros(far_tables.shape, jnp.float32)
    for g in range(groups):
        for spot, source in enumerate((far_columns_ref, far_rows_ref, far_rank_ref)):
            value = source[g : g + 1]
            if source is far_rows_ref:
                value = value - g * blocks
            far_tables[g, spot : spot + 1, : source.shape[1]] = value.astype(jnp.float32)

    out_recv()
    table = landed[:, top, :]
    total = jnp.sum(table, axis=0, keepdims=True)
    norms = [
        jnp.sqrt(single(total, capacity + s) / panels + epsilon) for s in range(sides)
    ]
    spread_marks = jnp.dot(
        one_hot(lax.div(iota((slots, count), 0), capacity) == iota((slots, count), 1)),
        jnp.where(iota((count, LANES), 1) < capacity, table, 0.0).astype(jnp.bfloat16),
        preferred_element_type=jnp.float32,
    )
    wide = (slots, LANES)
    held = jnp.sum(
        jnp.where(lax.rem(iota(wide, 0), capacity) == iota(wide, 1), spread_marks, 0.0),
        axis=1,
        keepdims=True,
    ).astype(jnp.int32) - 1
    to_mesh_wide = jnp.where(held == iota((slots, blocks), 1), 1.0, 0.0)
    to_mesh = to_mesh_wide.astype(jnp.bfloat16)
    to_cluster = to_mesh_wide.T.astype(jnp.bfloat16)
    for s in range(sides):
        arrived = landed[:, s * capacity : (s + 1) * capacity, :].reshape(slots, LANES)
        value = split_dot(to_cluster, arrived) / norms[s]
        first_ref[:, lanes[s]] = value
        own[:, lanes[s]] = value.astype(jnp.bfloat16)
    out_send()

    def operate(a, between):
        after = coordinates(lax.rem(me + 1, count), columns)
        before = coordinates(lax.rem(me + count - 1, count), columns)
        halos = [
            remote(
                own.at[pl.ds(blocks - halo, halo)],
                left,
                halo_send.at[a],
                halo_recv.at[a],
                0,
                after,
            ),
            remote(own.at[pl.ds(0, halo)], right, halo_send.at[a], halo_recv.at[a], 1, before),
        ]
        for copy in halos:
            copy.start()
        everything[row] = own[...]

        def inside(index):
            return (index >= 0) & (index < rows)

        def hop(way, distance, slot):
            sign = 1 - 2 * way
            return remote(
                everything.at[slot],
                everything.at[slot],
                spread_send.at[a, way],
                spread_recv.at[a, way],
                distance,
                (lax.rem(row + sign + rows, rows), column),
            )

        def relay(distance):
            for way in range(2):
                sign = 1 - 2 * way
                source = row - sign * distance
                if distance > 0:

                    @pl.when(inside(source))
                    def _(way=way, source=source):
                        hop(way, distance - 1, source).wait_recv()

                if distance < rows - 1:

                    @pl.when(inside(source) & inside(row + sign))
                    def _(way=way, source=source):
                        hop(way, distance, source).start()

        relay(0)
        image[...] = 0.5 * own[...].astype(jnp.float32)
        extended[halo : halo + blocks] = own[...]
        for copy in halos:
            copy.wait()
        extended[0:halo] = left[...]
        extended[halo + blocks :] = right[...]

        @pl.loop(0, near_groups)
        def _(g):
            if a == 0:
                load(0, g).wait()
            near_group(sides, g, near_tables, extended, near_ref, near_out, image)
            for distance in range(1, rows - 1):

                @pl.when(g == distance * near_groups // (rows - 1))
                def _(distance=distance):
                    relay(distance)

        relay(rows - 1)
        for way in range(2):
            sign = 1 - 2 * way
            for distance in range(rows - 1):
                source = row - sign * distance

                @pl.when(inside(source) & inside(row + sign))
                def _(way=way, source=source, distance=distance):
                    hop(way, distance, source).wait_send()

        between()
        if a == 0:
            for kind in (1, 2):

                @pl.loop(0, groups)
                def _(g, kind=kind):
                    load(kind, g).wait()

        far = functools.partial(
            far_group,
            sides,
            tables_ref=far_tables,
            everything=everything,
            far_left=far_left,
            far_right=far_right,
            far_out=far_out,
        )

        def pair_copy(k, q):
            return remote(
                to_partner.at[q],
                from_partner.at[q],
                pair_send.at[a],
                pair_recv.at[a],
                k,
                (row, partner),
            )

        def chip_copies(k, q, here):
            device = (row, 2 * q + core)
            if a == 0:
                return [
                    remote(
                        to_chips.at[q],
                        from_chips.at[here],
                        chip_send.at[a],
                        chip_recv.at[a],
                        k,
                        device,
                    )
                ]
            return [
                remote(
                    code_to.at[q],
                    code_from.at[here],
                    chip_send.at[a],
                    chip_recv.at[a],
                    k,
                    device,
                ),
                remote(scale_to.at[q], scale_from.at[here], scale_send, scale_recv, k, device),
            ]

        @pl.loop(1, pairs + 1)
        def _(i):
            q = lax.rem(chip + i, pairs)
            k = i - 1
            to_partner[q] = far(2 * q + 1 - core)
            pair_copy(k, q).start()
            to_chips[q] = far(2 * q + core)
            pair_copy(k, q).wait_recv()
            to_chips[q] = to_chips[q] + from_partner[q]

            @pl.when(i < pairs)
            def _():
                if a == 1:
                    for s in range(sides):
                        value = to_chips[q, :, lanes[s]]
                        scale = jnp.max(jnp.abs(value), axis=0, keepdims=True)
                        scale = jnp.maximum(scale, 1e-30)
                        scale_to[q, s * TILE : (s + 1) * TILE] = jnp.broadcast_to(
                            scale, (TILE, LANES)
                        )
                        code_to[q, :, lanes[s]] = encode(value, scale)
                for copy in chip_copies(k, q, chip):
                    copy.start()

        image[...] += to_chips[chip]
        for i in range(1, pairs):
            source = lax.rem(chip + pairs - i, pairs)
            for copy in chip_copies(i - 1, source, source):
                copy.wait_recv()
            if a == 0:
                image[...] += from_chips[source]
            else:
                for s in range(sides):
                    scale = scale_from[source, s * TILE : s * TILE + 1] * (1.0 / TOP)
                    image[:, lanes[s]] += decode(code_from[source, :, lanes[s]]) * scale
        for i in range(1, pairs + 1):
            q = lax.rem(chip + i, pairs)
            pair_copy(i - 1, q).wait_send()
            if i < pairs:
                for copy in chip_copies(i - 1, q, chip):
                    copy.wait_send()

    def slot_codes(value, scales, buffer):
        for s in range(0, sides, 2):
            codes = []
            for side in (s, s + 1):
                code = jnp.floor(
                    jnp.clip(value[:, lanes[side]] * (TOP / scales[side]), -TOP, TOP) + 0.5
                )
                codes.append(split_dot(to_mesh, code, 2).reshape(count, capacity, LANES))
            both = jnp.concatenate(codes, axis=1)
            buffer[:, s * capacity : (s + 2) * capacity, :] = both.astype(jnp.int32).astype(
                jnp.int16
            )

    to_own = one_hot(
        turned_target[:, 0:1] * capacity + rank_column == iota((blocks, slots), 1)
    )
    to_source = one_hot(turned_target[:, 0:1] == iota((blocks, count), 1))

    def home(buffer, scales):
        values = []
        own_scales = split_dot(to_source, scales)
        for s in range(0, sides, 2):
            both = decode(buffer[:, s * capacity : (s + 2) * capacity, :])
            for side in (s, s + 1):
                code = both[:, (side - s) * capacity : (side - s + 1) * capacity]
                value = split_dot(to_own, code.reshape(slots, LANES), 2)
                values.append(value * (own_scales[:, side : side + 1] * (1.0 / TOP)))
        return values

    operate(0, lambda: None)
    found = [[] for _ in range(7)]
    for s in range(sides):
        one, two = first_ref[:, lanes[s]], image[:, lanes[s]]
        along, size = total_of(one * two), total_of(one * one)
        guess = jnp.where(size > 1e-30, along / jnp.maximum(size, 1e-30), 0.0)
        rest = two - guess * one
        for place, value in enumerate(
            (
                along,
                guess,
                total_of(one * rest),
                total_of(rest * rest),
                size,
                largest(two),
                largest(one),
            )
        ):
            found[place].append(value)
    table = share(0, [value for values in found for value in values])()
    total = jnp.sum(table, axis=0, keepdims=True)
    projects, seconds, basis_scale = [], [], jnp.zeros((count, LANES), jnp.float32)
    for s in range(sides):
        guess, cross, rest, size, top_image, top_first = [
            table[:, n * sides + s : n * sides + s + 1] for n in range(1, 7)
        ]
        project = single(total, s) / panels
        off = guess - project
        norm = jnp.sqrt(
            jnp.sum(rest + off * (2.0 * cross + off * size), axis=0, keepdims=True) / panels
            + epsilon
        )
        value = (image[:, lanes[s]] - project * first_ref[:, lanes[s]]) / norm
        basis[:, lanes[s]] = value
        own[:, lanes[s]] = value.astype(jnp.bfloat16)
        bound = (top_image + jnp.abs(project) * top_first) / norm
        basis_scale = basis_scale + jnp.where(iota((count, LANES), 1) == s, bound, 0.0)
        projects.append(project)
        seconds.append(norm)
    mine_scale = jnp.sum(
        jnp.where(iota((count, LANES), 0) == me, basis_scale, 0.0), axis=0, keepdims=True
    )
    every = pl.ds(0, sides * capacity)
    basis_start, basis_recv, basis_send = to_all(1, sent_basis, landed_basis, every)
    image_start, image_recv, image_send = to_all(2, sent_image, landed_image, every)

    def send_basis():
        slot_codes(basis[...], [single(mine_scale, s) for s in range(sides)], sent_basis)
        basis_start()

    operate(1, send_basis)
    scales = [largest(image[:, lanes[s]]) for s in range(sides)]
    slot_codes(image[...], scales, sent_image)
    image_start()
    values = []
    for source in (first_ref, basis):
        for s in range(sides):
            values.append(total_of(source[:, lanes[s]] * image[:, lanes[s]]))
    wait = share(1, values + scales)
    basis_recv()
    returned = home(landed_basis, basis_scale)
    for s in range(sides):
        basis_ref[stride[s], :] = returned[s]
    table = wait()
    total = jnp.sum(table, axis=0, keepdims=True) / panels
    ends = [[single(total, n * sides + s) for s in range(sides)] for n in range(2)]
    for place, found in enumerate((norms, projects, seconds, ends[0], ends[1])):
        line = jnp.zeros((1, LANES), jnp.float32)
        for s in range(sides):
            line = line + jnp.where(lane_row == s, found[s], 0.0)
        entries_ref[place : place + 1] = line[:, :sides]
    kept = iota((count, LANES), 1)
    image_scale = jnp.zeros((count, LANES), jnp.float32)
    for s in range(sides):
        image_scale = image_scale + jnp.where(
            kept == s, table[:, 2 * sides + s : 2 * sides + s + 1], 0.0
        )
    image_recv()
    landed_values = home(landed_image, image_scale)
    for s in range(sides):
        next_ref[stride[s], :] = (
            landed_values[s]
            - ends[0][s] * (side_ref[stride[s], :] / norms[s])
            - ends[1][s] * returned[s]
        )
    basis_send()
    image_send()


def body(
    right_side,
    cluster_of,
    near_rows,
    near_columns,
    near_blocks,
    far_rows,
    far_columns,
    far_rank,
    far_left,
    far_right,
):
    rows = lax.axis_size("row")
    columns = lax.axis_size("col")
    count = rows * columns
    blocks, sides, lanes = right_side.shape
    width = sides * lanes
    capacity = max(TILE, 2 * blocks // count)
    near_groups = near_rows.shape[0] // lanes
    near_blocks = near_blocks.reshape(near_groups, -1, *near_blocks.shape[1:])
    far_left = far_left.reshape(columns, -1, *far_left.shape[1:])
    far_right = far_right.reshape(columns, -1, *far_right.shape[1:])
    halo = blocks // 4
    pairs = columns // 2
    dma = pltpu.SemaphoreType.DMA
    real, half, code = jnp.float32, jnp.bfloat16, jnp.int16
    out_slots = (count, sides * capacity + TILE, lanes)
    code_slots = (count, sides * capacity, lanes)
    hbm = pl.BlockSpec(memory_space=pl.ANY)
    basis, following, entries = pl.pallas_call(
        functools.partial(arnoldi_kernel, rows, columns),
        out_shape=[
            jax.ShapeDtypeStruct((blocks * sides, lanes), real),
            jax.ShapeDtypeStruct((blocks * sides, lanes), real),
            jax.ShapeDtypeStruct((5, sides), real),
        ],
        in_specs=[VMEM] * 7 + [hbm] * 3,
        out_specs=[VMEM] * 3,
        scratch_shapes=[
            pltpu.VMEM((near_groups, 8, lanes), real),
            pltpu.VMEM((columns, 8, lanes), real),
            pltpu.VMEM(out_slots, real),
            pltpu.VMEM(out_slots, real),
            pltpu.VMEM(code_slots, code),
            pltpu.VMEM(code_slots, code),
            pltpu.VMEM(code_slots, code),
            pltpu.VMEM(code_slots, code),
            pltpu.VMEM((blocks, width), real),
            pltpu.VMEM(near_blocks.shape, half),
            pltpu.VMEM(far_left.shape, half),
            pltpu.VMEM(far_right.shape, half),
            pltpu.VMEM((blocks, width), half),
            pltpu.VMEM((blocks, width), real),
            pltpu.VMEM((blocks, width), real),
            pltpu.VMEM((rows, blocks, width), half),
            pltpu.VMEM((blocks + 2 * halo, width), half),
            pltpu.VMEM((halo, width), half),
            pltpu.VMEM((halo, width), half),
            pltpu.VMEM((near_blocks.shape[1], width), real),
            pltpu.VMEM((far_left.shape[1], width), real),
            pltpu.VMEM((pairs, blocks, width), real),
            pltpu.VMEM((pairs, blocks, width), real),
            pltpu.VMEM((pairs, blocks, width), real),
            pltpu.VMEM((pairs, blocks, width), real),
            pltpu.VMEM((pairs, blocks, width), code),
            pltpu.VMEM((pairs, blocks, width), code),
            pltpu.VMEM((pairs, sides * TILE, lanes), real),
            pltpu.VMEM((pairs, sides * TILE, lanes), real),
            pltpu.VMEM((2, TILE, lanes), real),
            pltpu.VMEM((2, count, TILE, lanes), real),
            dma((3, max(columns, near_groups))),
            dma((2, 2)),
            dma((2, 2)),
            dma((2, 2, rows - 1)),
            dma((2, 2, rows - 1)),
            dma((2, pairs)),
            dma((2, pairs)),
            dma((2, pairs)),
            dma((2, pairs)),
            dma((pairs,)),
            dma((pairs,)),
            dma((5,)),
            dma((5,)),
        ],
        compiler_params=pltpu.CompilerParams(
            collective_id=0, has_side_effects=True, vmem_limit_bytes=LIMIT
        ),
    )(
        right_side.reshape(blocks * sides, lanes),
        cluster_of.reshape(1, blocks),
        near_columns.reshape(near_groups, -1),
        near_rows.reshape(near_groups, -1),
        far_columns.reshape(columns, -1),
        far_rows.reshape(columns, -1),
        far_rank.reshape(columns, -1),
        near_blocks,
        far_left,
        far_right,
    )
    shape = (blocks, sides, lanes)
    return (basis.reshape(shape), following.reshape(shape), entries)


def solution(mesh):
    vector = P(("row", "col"), None, None)
    table = P(("row", "col"))
    placed = (vector, table, table, table, vector, table, table, table, vector, vector)
    return jax.shard_map(
        body,
        mesh=mesh,
        in_specs=placed,
        out_specs=(vector, vector, P()),
        check_vma=False,
    )
```

```python
import functools

import jax
import jax.numpy as jnp
from jax import lax
from jax.experimental import pallas as pl
from jax.experimental.pallas import tpu as pltpu
from jax.sharding import PartitionSpec as P

epsilon = 1e-06
MESH = pl.DeviceIdType.MESH
VMEM = pl.BlockSpec(memory_space=pltpu.VMEM)
LANES = 128
LIMIT = 56 * 2**20
TILE = 8
TOP = 32767.0


def coordinates(index, column_count):
    return (lax.div(index, column_count), lax.rem(index, column_count))


def enter(me, rows, columns):
    count = rows * columns
    barrier = pltpu.get_barrier_semaphore()

    @pl.loop(1, count)
    def _(k):
        pl.semaphore_signal(
            barrier,
            inc=1,
            device_id=coordinates(lax.rem(me + k, count), columns),
            device_id_type=MESH,
        )

    pl.semaphore_wait(barrier, count - 1)


def split_dot(picker, value, terms=3):
    total = None
    for _ in range(terms):
        part = value.astype(jnp.bfloat16)
        value = value - part.astype(jnp.float32)
        product = jnp.dot(picker, part, preferred_element_type=jnp.float32)
        total = product if total is None else total + product
    return total


def one_hot(condition):
    return jnp.where(condition, 1.0, 0.0).astype(jnp.bfloat16)


def remote(source, destination, sends, recvs, k, device):
    return pltpu.make_async_remote_copy(
        src_ref=source,
        dst_ref=destination,
        send_sem=sends.at[k],
        recv_sem=recvs.at[k],
        device_id=device,
        device_id_type=MESH,
    )


def corners(one, two):
    empty = jnp.zeros_like(one)
    return jnp.concatenate(
        [jnp.concatenate([one, empty], axis=1), jnp.concatenate([empty, two], axis=1)], axis=0
    )


def near_group(sides, g, near_picked, near_place, near_ref, near_out, image, terms):
    near_count = near_ref.shape[1]
    half = 8
    both = 2 * half
    shape = (sides * half, LANES)
    row_id = lax.rem(lax.broadcasted_iota(jnp.int32, shape, 0), half)
    for j in range(near_count // both):
        here = [slice(j * both + n * half, j * both + (n + 1) * half) for n in range(2)]
        rows = [
            jnp.concatenate(
                [near_picked[g, here[n], s * LANES : (s + 1) * LANES] for s in range(sides)],
                axis=0,
            ).astype(jnp.bfloat16)
            for n in range(2)
        ]
        weights = jnp.concatenate(
            [near_ref[g, here[n]].reshape(half * LANES, LANES) for n in range(2)], axis=1
        )
        product = lax.dot_general(
            corners(*rows), weights, (((1,), (1,)), ((), ())), preferred_element_type=jnp.float32
        )
        for n in range(2):
            part = product[n * sides * half : (n + 1) * sides * half]
            value = part[:, :LANES]
            for e in range(1, half):
                value = jnp.where(row_id == e, part[:, e * LANES : (e + 1) * LANES], value)
            for s in range(sides):
                near_out[here[n], s * LANES : (s + 1) * LANES] = value[s * half : (s + 1) * half]
    image[...] += split_dot(near_place[g], near_out[...], terms)


def far_group(
    sides, terms, g, far_picked, far_place, far_ranks, far_left, far_right, far_out
):
    far_count, rank = far_left.shape[1:3]
    half = 16
    both = 2 * half
    shape = (sides * half, half * rank)
    entry = lax.rem(lax.broadcasted_iota(jnp.int32, shape, 0), half)
    lane = lax.broadcasted_iota(jnp.int32, shape, 1)
    term = lax.rem(lane, rank).astype(jnp.float32)
    own_entry = lax.div(lane, rank) == entry
    kept = []
    batches = [
        [slice(j * both + n * half, j * both + (n + 1) * half) for n in range(2)]
        for j in range(far_count // both)
    ]

    def weights(factor, here):
        return jnp.concatenate(
            [factor[g, part].reshape(half * rank, LANES) for part in here], axis=1
        )

    for here in batches:
        rows = [
            jnp.concatenate(
                [far_picked[g, part, s * LANES : (s + 1) * LANES] for s in range(sides)], axis=0
            )
            for part in here
        ]
        product = lax.dot_general(
            corners(*rows),
            weights(far_right, here),
            (((1,), (1,)), ((), ())),
            preferred_element_type=jnp.float32,
        )
        parts = []
        for n in range(2):
            ranks = jnp.concatenate([far_ranks[g, here[n], 0:1]] * sides, axis=0)
            part = product[n * sides * half : (n + 1) * sides * half]
            parts.append(jnp.where(own_entry & (term < ranks), part, 0.0).astype(jnp.bfloat16))
        kept.append(jnp.concatenate(parts, axis=0))
    for here, coefficients in zip(batches, kept):
        value = jnp.dot(coefficients, weights(far_left, here), preferred_element_type=jnp.float32)
        for n in range(2):
            part = value[n * sides * half : (n + 1) * sides * half, n * LANES : (n + 1) * LANES]
            for s in range(sides):
                far_out[here[n], s * LANES : (s + 1) * LANES] = part[s * half : (s + 1) * half]
    return split_dot(far_place[g], far_out[...], terms)


def iota(shape, dimension):
    return lax.broadcasted_iota(jnp.int32, shape, dimension)


def encode(value, scale):
    code = jnp.floor(jnp.clip(value * (TOP / scale), -TOP, TOP) + 0.5)
    return code.astype(jnp.int32).astype(jnp.int16)


def decode(code):
    return code.astype(jnp.int32).astype(jnp.float32)


def largest(value):
    top = jnp.max(jnp.abs(value), axis=0, keepdims=True)
    return jnp.maximum(jnp.max(top, axis=1, keepdims=True), 1e-30)


def total_of(value):
    return jnp.sum(jnp.sum(value, axis=0, keepdims=True), axis=1, keepdims=True)


def arnoldi_kernel(
    rows,
    columns,
    side_ref,
    cluster_ref,
    near_columns_ref,
    near_rows_ref,
    far_columns_ref,
    far_rows_ref,
    far_rank_ref,
    near_hbm,
    far_left_hbm,
    far_right_hbm,
    basis_ref,
    basis_rest_ref,
    next_ref,
    next_rest_ref,
    entries_ref,
    tables,
    near_pick,
    near_place,
    near_picked,
    far_pick,
    far_place,
    far_ranks,
    far_picked,
    sent,
    landed,
    sent_basis,
    landed_basis,
    sent_image,
    landed_image,
    first_ref,
    near_ref,
    far_left,
    far_right,
    own,
    basis,
    image,
    everything,
    extended,
    left,
    right,
    near_out,
    far_out,
    to_partner,
    from_partner,
    to_chips,
    from_chips,
    code_to,
    code_from,
    scale_to,
    scale_from,
    mine,
    parts,
    load_sem,
    halo_send,
    halo_recv,
    spread_send,
    spread_recv,
    pair_send,
    pair_recv,
    chip_send,
    chip_recv,
    scale_send,
    scale_recv,
    all_send,
    all_recv,
):
    row, column = lax.axis_index("row"), lax.axis_index("col")
    count = rows * columns
    me = row * columns + column
    blocks, width = first_ref.shape
    sides = width // LANES
    halo = left.shape[0]
    groups = far_left.shape[0]
    near_groups = near_ref.shape[0]
    pairs = columns // 2
    chip, core = lax.div(column, 2), lax.rem(column, 2)
    partner = 2 * chip + 1 - core
    panels = count * blocks * LANES
    lanes = [slice(s * LANES, (s + 1) * LANES) for s in range(sides)]
    capacity = (sent.shape[1] - TILE) // sides
    slots = count * capacity
    lane_row = iota((1, LANES), 1)

    def load(kind, g):
        source, target = (
            (near_hbm, near_ref),
            (far_left_hbm, far_left),
            (far_right_hbm, far_right),
        )[kind]
        return pltpu.make_async_copy(source.at[g], target.at[g], load_sem.at[kind, g])

    for kind, many in enumerate((near_groups, groups, groups)):

        @pl.loop(0, many)
        def _(g, kind=kind):
            load(kind, g).start()

    def to_all(n, source, destination, part):
        def copy(peer, there, here):
            return pltpu.make_async_remote_copy(
                src_ref=source.at[there, part],
                dst_ref=destination.at[here, part],
                send_sem=all_send.at[n],
                recv_sem=all_recv.at[n],
                device_id=coordinates(peer, columns),
                device_id_type=MESH,
            )

        def start():
            @pl.loop(1, count)
            def _(k):
                peer = lax.rem(me + k, count)
                copy(peer, peer, me).start()

            destination[me] = source[me]

        every = copy(lax.rem(me + 1, count), pl.ds(0, count - 1), pl.ds(0, count - 1))
        return start, every.wait_recv, every.wait_send

    def share(n, values):
        row_of = jnp.zeros((1, LANES), jnp.float32)
        for place, value in enumerate(values):
            row_of = row_of + jnp.where(lane_row == place, value, 0.0)
        mine[n] = jnp.broadcast_to(row_of, (TILE, LANES))

        def copy(peer, here):
            return pltpu.make_async_remote_copy(
                src_ref=(
                    parts.at[n, pl.ds(0, count - 1), pl.ds(0, 1)]
                    if here is None
                    else mine.at[n, pl.ds(0, 1)]
                ),
                dst_ref=parts.at[n, pl.ds(0, count - 1) if here is None else here, pl.ds(0, 1)],
                send_sem=all_send.at[3 + n],
                recv_sem=all_recv.at[3 + n],
                device_id=coordinates(peer, columns),
                device_id_type=MESH,
            )

        @pl.loop(1, count)
        def _(k):
            copy(lax.rem(me + k, count), me).start()

        parts[n, me] = mine[n]
        every = copy(lax.rem(me + 1, count), None)

        def wait():
            every.wait_recv()
            every.wait_send()
            return parts[n, :, 0, :]

        return wait

    def single(total, place):
        return jnp.sum(jnp.where(lane_row == place, total, 0.0), axis=1, keepdims=True)

    cluster = cluster_ref[...]
    target = lax.div(cluster, blocks)
    turned = jnp.broadcast_to(cluster.astype(jnp.float32), (blocks, blocks)).T.astype(jnp.int32)
    turned_target = lax.div(turned, blocks)
    place = turned - turned_target * blocks
    square = (blocks, blocks)
    same = turned_target == target
    ranks = jnp.where(same & (iota(square, 1) < iota(square, 0)), 1, 0)
    rank_column = jnp.sum(ranks, axis=1, keepdims=True)
    ranks = jnp.where(same & (iota(square, 0) < iota(square, 1)), 1, 0)
    rank_row = jnp.sum(ranks, axis=0, keepdims=True)
    slot_shape = (slots, blocks)
    to_slot = one_hot(iota(slot_shape, 0) == target * capacity + rank_row)
    to_device = one_hot(lax.div(iota(slot_shape, 0), capacity) == target)
    marks = jnp.where(iota(square, 1) == rank_column, place + 1, 0)
    extra = jnp.dot(
        to_device,
        marks.astype(jnp.float32).astype(jnp.bfloat16),
        preferred_element_type=jnp.float32,
    )
    stride = [pl.ds(s, blocks, stride=sides) for s in range(sides)]
    for s in range(sides):
        value = side_ref[stride[s], :]
        extra = extra + jnp.where(lane_row == capacity + s, total_of(value * value), 0.0)
        picked = split_dot(to_slot, value)
        sent[:, s * capacity : (s + 1) * capacity, :] = picked.reshape(count, capacity, LANES)
    top = sides * capacity
    if capacity == TILE:
        sent[:, top:, :] = extra.reshape(count, TILE, LANES)
    else:
        sent[:, top:, :] = extra.reshape(count, capacity, LANES)[:, :TILE]
    enter(me, rows, columns)
    out_start, out_recv, out_send = to_all(0, sent, landed, pl.ds(0, top + 1))
    out_start()

    near_count, far_count = near_ref.shape[1], far_left.shape[1]

    def turn(g, *sources):
        tables[g] = jnp.zeros(tables.shape[1:], jnp.float32)
        for spot, source in enumerate(sources):
            tables[g, spot : spot + 1, : source.shape[1]] = source.astype(jnp.float32)
        return tables[g].T

    def matches(column, many):
        return one_hot(column == iota((column.shape[0], many), 1).astype(jnp.float32))

    def places(row_of):
        return one_hot(iota((blocks, row_of.shape[1]), 0) == row_of)

    for g in range(near_groups):
        column_of = turn(g, near_columns_ref[g : g + 1])
        near_pick[g] = matches(column_of[:near_count, 0:1], extended.shape[0])
        near_place[g] = places(near_rows_ref[g : g + 1])
    for g in range(groups):
        column_of = turn(near_groups + g, far_columns_ref[g : g + 1], far_rank_ref[g : g + 1])
        far_pick[g] = matches(column_of[:far_count, 0:1], rows * blocks)
        far_ranks[g] = jnp.broadcast_to(column_of[:far_count, 1:2], far_ranks.shape[1:])
        far_place[g] = places(far_rows_ref[g : g + 1] - g * blocks)

    out_recv()
    table = landed[:, top, :]
    total = jnp.sum(table, axis=0, keepdims=True)
    norms = [
        jnp.sqrt(single(total, capacity + s) / panels + epsilon) for s in range(sides)
    ]
    spread_marks = jnp.dot(
        one_hot(lax.div(iota((slots, count), 0), capacity) == iota((slots, count), 1)),
        jnp.where(iota((count, LANES), 1) < capacity, table, 0.0).astype(jnp.bfloat16),
        preferred_element_type=jnp.float32,
    )
    wide = (slots, LANES)
    held = jnp.sum(
        jnp.where(lax.rem(iota(wide, 0), capacity) == iota(wide, 1), spread_marks, 0.0),
        axis=1,
        keepdims=True,
    ).astype(jnp.int32) - 1
    to_mesh_wide = jnp.where(held == iota((slots, blocks), 1), 1.0, 0.0)
    to_mesh = to_mesh_wide.astype(jnp.bfloat16)
    to_cluster = to_mesh_wide.T.astype(jnp.bfloat16)
    for s in range(sides):
        arrived = landed[:, s * capacity : (s + 1) * capacity, :].reshape(slots, LANES)
        value = split_dot(to_cluster, arrived) / norms[s]
        first_ref[:, lanes[s]] = value
        own[:, lanes[s]] = value.astype(jnp.bfloat16)
    out_send()

    def operate(a, between):
        after = coordinates(lax.rem(me + 1, count), columns)
        before = coordinates(lax.rem(me + count - 1, count), columns)
        halos = [
            remote(
                own.at[pl.ds(blocks - halo, halo)],
                left,
                halo_send.at[a],
                halo_recv.at[a],
                0,
                after,
            ),
            remote(own.at[pl.ds(0, halo)], right, halo_send.at[a], halo_recv.at[a], 1, before),
        ]
        for copy in halos:
            copy.start()
        everything[row] = own[...]

        def inside(index):
            return (index >= 0) & (index < rows)

        def hop(way, distance, source):
            sign = 1 - 2 * way
            reach = 2 if distance == 2 else 1
            return remote(
                everything.at[source],
                everything.at[source],
                spread_send.at[a, way],
                spread_recv.at[a, way],
                distance - 1,
                (lax.rem(row + sign * reach + 2 * rows, rows), column),
            )

        def arrive(distance):
            for way in range(2):
                source = row - (1 - 2 * way) * distance

                @pl.when(inside(source))
                def _(way=way, source=source):
                    hop(way, distance, source).wait_recv()

        def each_hop(distance, act):
            for way in range(2):
                sign = 1 - 2 * way
                held_at = 0 if distance < 3 else distance - 1
                source = row - sign * held_at
                there = row + sign * (2 if distance == 2 else 1)

                @pl.when(inside(source) & inside(there))
                def _(way=way, source=source):
                    act(hop(way, distance, source))

        each_hop(1, lambda copy: copy.start())
        if rows > 2:
            each_hop(2, lambda copy: copy.start())
        image[...] = 0.5 * own[...].astype(jnp.float32)
        extended[halo : halo + blocks] = own[...]
        for copy in halos:
            copy.wait()
        extended[0:halo] = left[...]
        extended[halo + blocks :] = right[...]
        for g in range(near_groups):
            near_picked[g] = jnp.dot(
                near_pick[g], extended[...], preferred_element_type=jnp.float32
            )

        @pl.loop(0, near_groups)
        def _(g):
            if a == 0:
                load(0, g).wait()
            near_group(sides, g, near_picked, near_place, near_ref, near_out, image, 3 - a)

        for distance in range(3, rows):
            arrive(distance - 1)
            each_hop(distance, lambda copy: copy.start())
        for distance in sorted({1, rows - 1}):
            arrive(distance)
        for distance in range(1, rows):
            each_hop(distance, lambda copy: copy.wait_send())
        between()
        if a == 0:
            for kind in (1, 2):

                @pl.loop(0, groups)
                def _(g, kind=kind):
                    load(kind, g).wait()

        for g in range(groups):
            far_picked[g] = jnp.dot(
                far_pick[g],
                everything[...].reshape(rows * blocks, width),
                preferred_element_type=jnp.float32,
            ).astype(jnp.bfloat16)

        far = functools.partial(
            far_group,
            sides,
            3 - a,
            far_picked=far_picked,
            far_place=far_place,
            far_ranks=far_ranks,
            far_left=far_left,
            far_right=far_right,
            far_out=far_out,
        )

        def pair_copy(k, q):
            return remote(
                to_partner.at[q],
                from_partner.at[q],
                pair_send.at[a],
                pair_recv.at[a],
                k,
                (row, partner),
            )

        def chip_copies(k, q, here):
            device = (row, 2 * q + core)
            if a == 0:
                return [
                    remote(
                        to_chips.at[q],
                        from_chips.at[here],
                        chip_send.at[a],
                        chip_recv.at[a],
                        k,
                        device,
                    )
                ]
            return [
                remote(
                    code_to.at[q],
                    code_from.at[here],
                    chip_send.at[a],
                    chip_recv.at[a],
                    k,
                    device,
                ),
                remote(scale_to.at[q], scale_from.at[here], scale_send, scale_recv, k, device),
            ]

        @pl.loop(1, pairs + 1)
        def _(i):
            q = lax.rem(chip + i, pairs)
            to_partner[q] = far(2 * q + 1 - core)
            pair_copy(i - 1, q).start()

        @pl.loop(1, pairs + 1)
        def _(i):
            q = lax.rem(chip + i, pairs)
            k = i - 1
            to_chips[q] = far(2 * q + core)
            pair_copy(k, q).wait_recv()
            to_chips[q] = to_chips[q] + from_partner[q]

            @pl.when(i < pairs)
            def _():
                if a == 1:
                    for s in range(sides):
                        value = to_chips[q, :, lanes[s]]
                        scale = jnp.max(jnp.abs(value), axis=0, keepdims=True)
                        scale = jnp.maximum(scale, 1e-30)
                        scale_to[q, s * TILE : (s + 1) * TILE] = jnp.broadcast_to(
                            scale, (TILE, LANES)
                        )
                        code_to[q, :, lanes[s]] = encode(value, scale)
                for copy in chip_copies(k, q, chip):
                    copy.start()

        image[...] += to_chips[chip]
        for i in range(1, pairs):
            source = lax.rem(chip + pairs - i, pairs)
            for copy in chip_copies(i - 1, source, source):
                copy.wait_recv()
            if a == 0:
                image[...] += from_chips[source]
            else:
                for s in range(sides):
                    scale = scale_from[source, s * TILE : s * TILE + 1] * (1.0 / TOP)
                    image[:, lanes[s]] += decode(code_from[source, :, lanes[s]]) * scale
        for i in range(1, pairs + 1):
            q = lax.rem(chip + i, pairs)
            pair_copy(i - 1, q).wait_send()
            if i < pairs:
                for copy in chip_copies(i - 1, q, chip):
                    copy.wait_send()

    def slot_codes(value, scales, buffer):
        for s in range(0, sides, 2):
            codes = []
            for side in (s, s + 1):
                code = jnp.floor(
                    jnp.clip(value[:, lanes[side]] * (TOP / scales[side]), -TOP, TOP) + 0.5
                )
                codes.append(split_dot(to_mesh, code, 2).reshape(count, capacity, LANES))
            both = jnp.concatenate(codes, axis=1)
            buffer[:, s * capacity : (s + 2) * capacity, :] = both.astype(jnp.int32).astype(
                jnp.int16
            )

    to_own = one_hot(
        turned_target[:, 0:1] * capacity + rank_column == iota((blocks, slots), 1)
    )
    to_source = one_hot(turned_target[:, 0:1] == iota((blocks, count), 1))

    def home(buffer, scales):
        values = []
        own_scales = split_dot(to_source, scales)
        for s in range(0, sides, 2):
            both = decode(buffer[:, s * capacity : (s + 2) * capacity, :])
            for side in (s, s + 1):
                code = both[:, (side - s) * capacity : (side - s + 1) * capacity]
                code = code.reshape(slots, LANES)
                high = code.astype(jnp.bfloat16)
                scale = own_scales[:, side : side + 1] * (1.0 / TOP)
                values.append(
                    (
                        split_dot(to_own, high, 1) * scale,
                        split_dot(to_own, code - high.astype(jnp.float32), 1) * scale,
                    )
                )
        return values

    operate(0, lambda: None)
    found = [[] for _ in range(7)]
    for s in range(sides):
        one, two = first_ref[:, lanes[s]], image[:, lanes[s]]
        along, size = total_of(one * two), total_of(one * one)
        guess = jnp.where(size > 1e-30, along / jnp.maximum(size, 1e-30), 0.0)
        rest = two - guess * one
        for place, value in enumerate(
            (
                along,
                guess,
                total_of(one * rest),
                total_of(rest * rest),
                size,
                largest(two),
                largest(one),
            )
        ):
            found[place].append(value)
    table = share(0, [value for values in found for value in values])()
    total = jnp.sum(table, axis=0, keepdims=True)
    projects, seconds, basis_scale = [], [], jnp.zeros((count, LANES), jnp.float32)
    for s in range(sides):
        guess, cross, rest, size, top_image, top_first = [
            table[:, n * sides + s : n * sides + s + 1] for n in range(1, 7)
        ]
        project = single(total, s) / panels
        off = guess - project
        norm = jnp.sqrt(
            jnp.sum(rest + off * (2.0 * cross + off * size), axis=0, keepdims=True) / panels
            + epsilon
        )
        value = (image[:, lanes[s]] - project * first_ref[:, lanes[s]]) / norm
        basis[:, lanes[s]] = value
        own[:, lanes[s]] = value.astype(jnp.bfloat16)
        bound = (top_image + jnp.abs(project) * top_first) / norm
        basis_scale = basis_scale + jnp.where(iota((count, LANES), 1) == s, bound, 0.0)
        projects.append(project)
        seconds.append(norm)
    mine_scale = jnp.sum(
        jnp.where(iota((count, LANES), 0) == me, basis_scale, 0.0), axis=0, keepdims=True
    )
    every = pl.ds(0, sides * capacity)
    basis_start, basis_recv, basis_send = to_all(1, sent_basis, landed_basis, every)
    image_start, image_recv, image_send = to_all(2, sent_image, landed_image, every)

    def send_basis():
        slot_codes(basis[...], [single(mine_scale, s) for s in range(sides)], sent_basis)
        basis_start()

    operate(1, send_basis)
    scales = [largest(image[:, lanes[s]]) for s in range(sides)]
    slot_codes(image[...], scales, sent_image)
    image_start()
    values = []
    for source in (first_ref, basis):
        for s in range(sides):
            values.append(total_of(source[:, lanes[s]] * image[:, lanes[s]]))
    wait = share(1, values + scales)
    basis_recv()
    returned = home(landed_basis, basis_scale)
    for s in range(sides):
        basis_ref[stride[s], :], basis_rest_ref[stride[s], :] = returned[s]
    table = wait()
    total = jnp.sum(table, axis=0, keepdims=True) / panels
    ends = [[single(total, n * sides + s) for s in range(sides)] for n in range(2)]
    for s in range(sides):
        line = jnp.zeros((1, LANES), jnp.float32)
        for place, found in enumerate((norms, projects, seconds, ends[0], ends[1])):
            line = line + jnp.where(lane_row == place, found[s], 0.0)
        entries_ref[s : s + 1] = line[:, : entries_ref.shape[1]]
    kept = iota((count, LANES), 1)
    image_scale = jnp.zeros((count, LANES), jnp.float32)
    for s in range(sides):
        image_scale = image_scale + jnp.where(
            kept == s, table[:, 2 * sides + s : 2 * sides + s + 1], 0.0
        )
    image_recv()
    landed_values = home(landed_image, image_scale)
    for s in range(sides):
        high, rest = landed_values[s]
        next_ref[stride[s], :] = high + rest - ends[0][s] * (side_ref[stride[s], :] / norms[s])
        next_rest_ref[stride[s], :] = ends[1][s] * (returned[s][0] + returned[s][1])
    basis_send()
    image_send()


def body(
    right_side,
    cluster_of,
    near_rows,
    near_columns,
    near_blocks,
    far_rows,
    far_columns,
    far_rank,
    far_left,
    far_right,
):
    rows = lax.axis_size("row")
    columns = lax.axis_size("col")
    count = rows * columns
    blocks, sides, lanes = right_side.shape
    width = sides * lanes
    capacity = max(TILE, 2 * blocks // count)
    near_groups = near_rows.shape[0] // lanes
    near_blocks = near_blocks.reshape(near_groups, -1, *near_blocks.shape[1:])
    far_left = far_left.reshape(columns, -1, *far_left.shape[1:])
    far_right = far_right.reshape(columns, -1, *far_right.shape[1:])
    near_count, far_count = near_blocks.shape[1], far_left.shape[1]
    halo = blocks // 4
    pairs = columns // 2
    dma = pltpu.SemaphoreType.DMA
    real, half, code = jnp.float32, jnp.bfloat16, jnp.int16
    out_slots = (count, sides * capacity + TILE, lanes)
    code_slots = (count, sides * capacity, lanes)
    hbm = pl.BlockSpec(memory_space=pl.ANY)
    basis, basis_rest, following, following_rest, entries = pl.pallas_call(
        functools.partial(arnoldi_kernel, rows, columns),
        out_shape=[
            *[jax.ShapeDtypeStruct((blocks * sides, lanes), real)] * 4,
            jax.ShapeDtypeStruct((sides, 5), real),
        ],
        in_specs=[VMEM] * 7 + [hbm] * 3,
        out_specs=[VMEM] * 5,
        scratch_shapes=[
            pltpu.VMEM((near_groups + columns, TILE, lanes), real),
            pltpu.VMEM((near_groups, near_count, blocks + 2 * halo), half),
            pltpu.VMEM((near_groups, blocks, near_count), half),
            pltpu.VMEM((near_groups, near_count, width), real),
            pltpu.VMEM((columns, far_count, rows * blocks), half),
            pltpu.VMEM((columns, blocks, far_count), half),
            pltpu.VMEM((columns, far_count, lanes), real),
            pltpu.VMEM((columns, far_count, width), half),
            pltpu.VMEM(out_slots, real),
            pltpu.VMEM(out_slots, real),
            pltpu.VMEM(code_slots, code),
            pltpu.VMEM(code_slots, code),
            pltpu.VMEM(code_slots, code),
            pltpu.VMEM(code_slots, code),
            pltpu.VMEM((blocks, width), real),
            pltpu.VMEM(near_blocks.shape, half),
            pltpu.VMEM(far_left.shape, half),
            pltpu.VMEM(far_right.shape, half),
            pltpu.VMEM((blocks, width), half),
            pltpu.VMEM((blocks, width), real),
            pltpu.VMEM((blocks, width), real),
            pltpu.VMEM((rows, blocks, width), half),
            pltpu.VMEM((blocks + 2 * halo, width), half),
            pltpu.VMEM((halo, width), half),
            pltpu.VMEM((halo, width), half),
            pltpu.VMEM((near_blocks.shape[1], width), real),
            pltpu.VMEM((far_left.shape[1], width), real),
            pltpu.VMEM((pairs, blocks, width), real),
            pltpu.VMEM((pairs, blocks, width), real),
            pltpu.VMEM((pairs, blocks, width), real),
            pltpu.VMEM((pairs, blocks, width), real),
            pltpu.VMEM((pairs, blocks, width), code),
            pltpu.VMEM((pairs, blocks, width), code),
            pltpu.VMEM((pairs, sides * TILE, lanes), real),
            pltpu.VMEM((pairs, sides * TILE, lanes), real),
            pltpu.VMEM((2, TILE, lanes), real),
            pltpu.VMEM((2, count, TILE, lanes), real),
            dma((3, max(columns, near_groups))),
            dma((2, 2)),
            dma((2, 2)),
            dma((2, 2, rows - 1)),
            dma((2, 2, rows - 1)),
            dma((2, pairs)),
            dma((2, pairs)),
            dma((2, pairs)),
            dma((2, pairs)),
            dma((pairs,)),
            dma((pairs,)),
            dma((5,)),
            dma((5,)),
        ],
        compiler_params=pltpu.CompilerParams(
            collective_id=0, has_side_effects=True, vmem_limit_bytes=LIMIT
        ),
    )(
        right_side.reshape(blocks * sides, lanes),
        cluster_of.reshape(1, blocks),
        near_columns.reshape(near_groups, -1),
        near_rows.reshape(near_groups, -1),
        far_columns.reshape(columns, -1),
        far_rows.reshape(columns, -1),
        far_rank.reshape(columns, -1),
        near_blocks,
        far_left,
        far_right,
    )
    shape = (blocks, sides, lanes)
    return (
        (basis + basis_rest).reshape(shape),
        (following - following_rest).reshape(shape),
        entries.T,
    )


def solution(mesh):
    vector = P(("row", "col"), None, None)
    table = P(("row", "col"))
    placed = (vector, table, table, table, vector, table, table, table, vector, vector)
    return jax.shard_map(
        body,
        mesh=mesh,
        in_specs=placed,
        out_specs=(vector, vector, P()),
        check_vma=False,
    )
```

```python
import functools

import jax
import jax.numpy as jnp
from jax import lax
from jax.experimental import pallas as pl
from jax.experimental.pallas import tpu as pltpu
from jax.sharding import PartitionSpec as P

epsilon = 1e-06
MESH = pl.DeviceIdType.MESH
VMEM = pl.BlockSpec(memory_space=pltpu.VMEM)
LANES = 128
LIMIT = 56 * 2**20
TILE = 8
TOP = 32767.0
WIDE = 8388607.0
BYTE = 256.0


def coordinates(index, column_count):
    return (lax.div(index, column_count), lax.rem(index, column_count))


def greet(me, rows, columns):
    count = rows * columns
    barrier = pltpu.get_barrier_semaphore()

    @pl.loop(1, count)
    def _(k):
        pl.semaphore_signal(
            barrier,
            inc=1,
            device_id=coordinates(lax.rem(me + k, count), columns),
            device_id_type=MESH,
        )

    return functools.partial(pl.semaphore_wait, barrier, count - 1)


def split_dot(picker, value, terms=3):
    total = None
    for _ in range(terms):
        part = value.astype(jnp.bfloat16)
        value = value - part.astype(jnp.float32)
        product = jnp.dot(picker, part, preferred_element_type=jnp.float32)
        total = product if total is None else total + product
    return total


def one_hot(condition):
    return jnp.where(condition, 1.0, 0.0).astype(jnp.bfloat16)


def remote(source, destination, sends, recvs, k, device):
    return pltpu.make_async_remote_copy(
        src_ref=source,
        dst_ref=destination,
        send_sem=sends.at[k],
        recv_sem=recvs.at[k],
        device_id=device,
        device_id_type=MESH,
    )


def corners(one, two):
    empty = jnp.zeros_like(one)
    return jnp.concatenate(
        [jnp.concatenate([one, empty], axis=1), jnp.concatenate([empty, two], axis=1)], axis=0
    )


def near_group(sides, g, near_picked, near_place, near_ref, near_out, image, terms):
    near_count = near_ref.shape[1]
    half = 8
    both = 2 * half
    shape = (sides * half, LANES)
    row_id = lax.rem(lax.broadcasted_iota(jnp.int32, shape, 0), half)
    for j in range(near_count // both):
        here = [slice(j * both + n * half, j * both + (n + 1) * half) for n in range(2)]
        rows = [
            jnp.concatenate(
                [near_picked[g, here[n], s * LANES : (s + 1) * LANES] for s in range(sides)],
                axis=0,
            ).astype(jnp.bfloat16)
            for n in range(2)
        ]
        weights = jnp.concatenate(
            [near_ref[g, here[n]].reshape(half * LANES, LANES) for n in range(2)], axis=1
        )
        product = lax.dot_general(
            corners(*rows), weights, (((1,), (1,)), ((), ())), preferred_element_type=jnp.float32
        )
        for n in range(2):
            part = product[n * sides * half : (n + 1) * sides * half]
            value = part[:, :LANES]
            for e in range(1, half):
                value = jnp.where(row_id == e, part[:, e * LANES : (e + 1) * LANES], value)
            for s in range(sides):
                near_out[here[n], s * LANES : (s + 1) * LANES] = value[s * half : (s + 1) * half]
    image[...] += split_dot(near_place[g], near_out[...], terms)


def far_group(
    sides, terms, g, far_picked, far_place, far_ranks, far_left, far_right, far_out
):
    far_count, rank = far_left.shape[1:3]
    half = 16
    both = 2 * half
    shape = (sides * half, half * rank)
    entry = lax.rem(lax.broadcasted_iota(jnp.int32, shape, 0), half)
    lane = lax.broadcasted_iota(jnp.int32, shape, 1)
    term = lax.rem(lane, rank).astype(jnp.float32)
    own_entry = lax.div(lane, rank) == entry
    kept = []
    batches = [
        [slice(j * both + n * half, j * both + (n + 1) * half) for n in range(2)]
        for j in range(far_count // both)
    ]

    def weights(factor, here):
        return jnp.concatenate(
            [factor[g, part].reshape(half * rank, LANES) for part in here], axis=1
        )

    for here in batches:
        rows = [
            jnp.concatenate(
                [far_picked[g, part, s * LANES : (s + 1) * LANES] for s in range(sides)], axis=0
            )
            for part in here
        ]
        product = lax.dot_general(
            corners(*rows),
            weights(far_right, here),
            (((1,), (1,)), ((), ())),
            preferred_element_type=jnp.float32,
        )
        parts = []
        for n in range(2):
            ranks = jnp.concatenate([far_ranks[g, here[n], 0:1]] * sides, axis=0)
            part = product[n * sides * half : (n + 1) * sides * half]
            parts.append(jnp.where(own_entry & (term < ranks), part, 0.0).astype(jnp.bfloat16))
        kept.append(jnp.concatenate(parts, axis=0))
    for here, coefficients in zip(batches, kept):
        value = jnp.dot(coefficients, weights(far_left, here), preferred_element_type=jnp.float32)
        for n in range(2):
            part = value[n * sides * half : (n + 1) * sides * half, n * LANES : (n + 1) * LANES]
            for s in range(sides):
                far_out[here[n], s * LANES : (s + 1) * LANES] = part[s * half : (s + 1) * half]
    return split_dot(far_place[g], far_out[...], terms)


def iota(shape, dimension):
    return lax.broadcasted_iota(jnp.int32, shape, dimension)


def to_code(value, scale, top):
    return jnp.floor(jnp.clip(value * (top / scale), -top, top) + 0.5)


def narrow(code):
    return code.astype(jnp.int32).astype(jnp.int16)


def decode(code):
    return code.astype(jnp.int32).astype(jnp.float32)


def largest(value):
    top = jnp.max(jnp.abs(value), axis=0, keepdims=True)
    return jnp.maximum(jnp.max(top, axis=1, keepdims=True), 1e-30)


def total_of(value):
    return jnp.sum(jnp.sum(value, axis=0, keepdims=True), axis=1, keepdims=True)


def arnoldi_kernel(
    rows,
    columns,
    side_ref,
    cluster_ref,
    near_columns_ref,
    near_rows_ref,
    far_columns_ref,
    far_rows_ref,
    far_rank_ref,
    near_hbm,
    far_left_hbm,
    far_right_hbm,
    basis_ref,
    basis_rest_ref,
    next_ref,
    next_rest_ref,
    entries_ref,
    tables,
    near_pick,
    near_place,
    near_picked,
    far_pick,
    far_place,
    far_ranks,
    far_picked,
    sent,
    landed,
    sent_basis,
    landed_basis,
    sent_image,
    landed_image,
    first_ref,
    near_ref,
    far_left,
    far_right,
    own,
    basis,
    image,
    everything,
    extended,
    left,
    right,
    near_out,
    far_out,
    to_partner,
    from_partner,
    to_chips,
    wide_to,
    wide_from,
    code_to,
    code_from,
    scale_to,
    scale_from,
    mine,
    parts,
    load_sem,
    halo_send,
    halo_recv,
    spread_send,
    spread_recv,
    pair_send,
    pair_recv,
    chip_send,
    chip_recv,
    scale_send,
    scale_recv,
    all_send,
    all_recv,
):
    row, column = lax.axis_index("row"), lax.axis_index("col")
    count = rows * columns
    me = row * columns + column
    blocks, width = first_ref.shape
    sides = width // LANES
    halo = left.shape[0]
    groups = far_left.shape[0]
    near_groups = near_ref.shape[0]
    pairs = columns // 2
    chip, core = lax.div(column, 2), lax.rem(column, 2)
    partner = 2 * chip + 1 - core
    panels = count * blocks * LANES
    lanes = [slice(s * LANES, (s + 1) * LANES) for s in range(sides)]
    capacity = (sent.shape[1] - TILE) // sides
    slots = count * capacity
    lane_row = iota((1, LANES), 1)
    code_to, code_from = (wide_to, code_to), (wide_from, code_from)
    entered = greet(me, rows, columns)

    def load(kind, g):
        source, target = (
            (near_hbm, near_ref),
            (far_left_hbm, far_left),
            (far_right_hbm, far_right),
        )[kind]
        return pltpu.make_async_copy(source.at[g], target.at[g], load_sem.at[kind, g])

    for kind, many in enumerate((near_groups, groups, groups)):

        @pl.loop(0, many)
        def _(g, kind=kind):
            load(kind, g).start()

    def to_all(n, source, destination, part):
        def copy(peer, there, here):
            return pltpu.make_async_remote_copy(
                src_ref=source.at[there, part],
                dst_ref=destination.at[here, part],
                send_sem=all_send.at[n],
                recv_sem=all_recv.at[n],
                device_id=coordinates(peer, columns),
                device_id_type=MESH,
            )

        def start():
            @pl.loop(1, count)
            def _(k):
                peer = lax.rem(me + k, count)
                copy(peer, peer, me).start()

            destination[me] = source[me]

        every = copy(lax.rem(me + 1, count), pl.ds(0, count - 1), pl.ds(0, count - 1))
        return start, every.wait_recv, every.wait_send

    def share(n, values):
        row_of = jnp.zeros((1, LANES), jnp.float32)
        for place, value in enumerate(values):
            row_of = row_of + jnp.where(lane_row == place, value, 0.0)
        mine[n] = jnp.broadcast_to(row_of, (TILE, LANES))

        def copy(peer, here):
            return pltpu.make_async_remote_copy(
                src_ref=(
                    parts.at[n, pl.ds(0, count - 1), pl.ds(0, 1)]
                    if here is None
                    else mine.at[n, pl.ds(0, 1)]
                ),
                dst_ref=parts.at[n, pl.ds(0, count - 1) if here is None else here, pl.ds(0, 1)],
                send_sem=all_send.at[3 + n],
                recv_sem=all_recv.at[3 + n],
                device_id=coordinates(peer, columns),
                device_id_type=MESH,
            )

        @pl.loop(1, count)
        def _(k):
            copy(lax.rem(me + k, count), me).start()

        parts[n, me] = mine[n]
        every = copy(lax.rem(me + 1, count), None)

        def wait():
            every.wait_recv()
            every.wait_send()
            return parts[n, :, 0, :]

        return wait

    def single(total, place):
        return jnp.sum(jnp.where(lane_row == place, total, 0.0), axis=1, keepdims=True)

    cluster = cluster_ref[...]
    target = lax.div(cluster, blocks)
    turned = jnp.broadcast_to(cluster.astype(jnp.float32), (blocks, blocks)).T.astype(jnp.int32)
    turned_target = lax.div(turned, blocks)
    place = turned - turned_target * blocks
    square = (blocks, blocks)
    same = turned_target == target
    ranks = jnp.where(same & (iota(square, 1) < iota(square, 0)), 1, 0)
    rank_column = jnp.sum(ranks, axis=1, keepdims=True)
    ranks = jnp.where(same & (iota(square, 0) < iota(square, 1)), 1, 0)
    rank_row = jnp.sum(ranks, axis=0, keepdims=True)
    slot_shape = (slots, blocks)
    to_slot = one_hot(iota(slot_shape, 0) == target * capacity + rank_row)
    to_device = one_hot(lax.div(iota(slot_shape, 0), capacity) == target)
    marks = jnp.where(iota(square, 1) == rank_column, place + 1, 0)
    extra = jnp.dot(
        to_device,
        marks.astype(jnp.float32).astype(jnp.bfloat16),
        preferred_element_type=jnp.float32,
    )
    stride = [pl.ds(s, blocks, stride=sides) for s in range(sides)]
    for s in range(sides):
        value = side_ref[stride[s], :]
        extra = extra + jnp.where(lane_row == capacity + s, total_of(value * value), 0.0)
        picked = split_dot(to_slot, value)
        sent[:, s * capacity : (s + 1) * capacity, :] = picked.reshape(count, capacity, LANES)
    top = sides * capacity
    if capacity == TILE:
        sent[:, top:, :] = extra.reshape(count, TILE, LANES)
    else:
        sent[:, top:, :] = extra.reshape(count, capacity, LANES)[:, :TILE]
    entered()
    out_start, out_recv, out_send = to_all(0, sent, landed, pl.ds(0, top + 1))
    out_start()

    near_count, far_count = near_ref.shape[1], far_left.shape[1]

    def turn(g, *sources):
        tables[g] = jnp.zeros(tables.shape[1:], jnp.float32)
        for spot, source in enumerate(sources):
            tables[g, spot : spot + 1, : source.shape[1]] = source.astype(jnp.float32)
        return tables[g].T

    def matches(column, many):
        return one_hot(column == iota((column.shape[0], many), 1).astype(jnp.float32))

    def places(row_of):
        return one_hot(iota((blocks, row_of.shape[1]), 0) == row_of)

    for g in range(near_groups):
        column_of = turn(g, near_columns_ref[g : g + 1])
        near_pick[g] = matches(column_of[:near_count, 0:1], extended.shape[0])
        near_place[g] = places(near_rows_ref[g : g + 1])
    for g in range(groups):
        column_of = turn(near_groups + g, far_columns_ref[g : g + 1], far_rank_ref[g : g + 1])
        far_pick[g] = matches(column_of[:far_count, 0:1], rows * blocks)
        far_ranks[g] = jnp.broadcast_to(column_of[:far_count, 1:2], far_ranks.shape[1:])
        far_place[g] = places(far_rows_ref[g : g + 1] - g * blocks)

    out_recv()
    table = landed[:, top, :]
    total = jnp.sum(table, axis=0, keepdims=True)
    norms = [
        jnp.sqrt(single(total, capacity + s) / panels + epsilon) for s in range(sides)
    ]
    spread_marks = jnp.dot(
        one_hot(lax.div(iota((slots, count), 0), capacity) == iota((slots, count), 1)),
        jnp.where(iota((count, LANES), 1) < capacity, table, 0.0).astype(jnp.bfloat16),
        preferred_element_type=jnp.float32,
    )
    wide = (slots, LANES)
    held = jnp.sum(
        jnp.where(lax.rem(iota(wide, 0), capacity) == iota(wide, 1), spread_marks, 0.0),
        axis=1,
        keepdims=True,
    ).astype(jnp.int32) - 1
    to_mesh_wide = jnp.where(held == iota((slots, blocks), 1), 1.0, 0.0)
    to_mesh = to_mesh_wide.astype(jnp.bfloat16)
    to_cluster = to_mesh_wide.T.astype(jnp.bfloat16)
    for s in range(sides):
        arrived = landed[:, s * capacity : (s + 1) * capacity, :].reshape(slots, LANES)
        value = split_dot(to_cluster, arrived) / norms[s]
        first_ref[:, lanes[s]] = value
        own[:, lanes[s]] = value.astype(jnp.bfloat16)
    out_send()

    def operate(a, between):
        after = coordinates(lax.rem(me + 1, count), columns)
        before = coordinates(lax.rem(me + count - 1, count), columns)
        halos = [
            remote(
                own.at[pl.ds(blocks - halo, halo)],
                left,
                halo_send.at[a],
                halo_recv.at[a],
                0,
                after,
            ),
            remote(own.at[pl.ds(0, halo)], right, halo_send.at[a], halo_recv.at[a], 1, before),
        ]
        for copy in halos:
            copy.start()
        everything[row] = own[...]

        def inside(index):
            return (index >= 0) & (index < rows)

        def hop(way, distance, source):
            sign = 1 - 2 * way
            reach = 2 if distance == 2 else 1
            return remote(
                everything.at[source],
                everything.at[source],
                spread_send.at[a, way],
                spread_recv.at[a, way],
                distance - 1,
                (lax.rem(row + sign * reach + 2 * rows, rows), column),
            )

        def arrive(distance):
            for way in range(2):
                source = row - (1 - 2 * way) * distance

                @pl.when(inside(source))
                def _(way=way, source=source):
                    hop(way, distance, source).wait_recv()

        def each_hop(distance, act):
            for way in range(2):
                sign = 1 - 2 * way
                held_at = 0 if distance < 3 else distance - 1
                source = row - sign * held_at
                there = row + sign * (2 if distance == 2 else 1)

                @pl.when(inside(source) & inside(there))
                def _(way=way, source=source):
                    act(hop(way, distance, source))

        each_hop(1, lambda copy: copy.start())
        if rows > 2:
            each_hop(2, lambda copy: copy.start())
        image[...] = 0.5 * own[...].astype(jnp.float32)
        extended[halo : halo + blocks] = own[...]
        for copy in halos:
            copy.wait()
        extended[0:halo] = left[...]
        extended[halo + blocks :] = right[...]
        for g in range(near_groups):
            near_picked[g] = jnp.dot(
                near_pick[g], extended[...], preferred_element_type=jnp.float32
            )

        @pl.loop(0, near_groups)
        def _(g):
            if a == 0:
                load(0, g).wait()
            near_group(sides, g, near_picked, near_place, near_ref, near_out, image, 3 - a)

        for distance in range(3, rows):
            arrive(distance - 1)
            each_hop(distance, lambda copy: copy.start())
        for distance in sorted({1, rows - 1}):
            arrive(distance)
        for distance in range(1, rows):
            each_hop(distance, lambda copy: copy.wait_send())
        between()
        if a == 0:
            for kind in (1, 2):

                @pl.loop(0, groups)
                def _(g, kind=kind):
                    load(kind, g).wait()

        for g in range(groups):
            far_picked[g] = jnp.dot(
                far_pick[g],
                everything[...].reshape(rows * blocks, width),
                preferred_element_type=jnp.float32,
            ).astype(jnp.bfloat16)

        far = functools.partial(
            far_group,
            sides,
            3 - a,
            far_picked=far_picked,
            far_place=far_place,
            far_ranks=far_ranks,
            far_left=far_left,
            far_right=far_right,
            far_out=far_out,
        )

        def pair_copy(k, q):
            return remote(
                to_partner.at[q],
                from_partner.at[q],
                pair_send.at[a],
                pair_recv.at[a],
                k,
                (row, partner),
            )

        def chip_copies(k, q, here):
            device = (row, 2 * q + core)
            return [
                remote(
                    code_to[a].at[q],
                    code_from[a].at[here],
                    chip_send.at[a],
                    chip_recv.at[a],
                    k,
                    device,
                ),
                remote(
                    scale_to.at[a, q],
                    scale_from.at[a, here],
                    scale_send.at[a],
                    scale_recv.at[a],
                    k,
                    device,
                ),
            ]

        top_code = WIDE if a == 0 else TOP

        def pack(source, q):
            lows = []
            for s in range(sides):
                value = source[q, :, lanes[s]]
                scale = jnp.maximum(jnp.max(jnp.abs(value), axis=0, keepdims=True), 1e-30)
                scale_to[a, q, s * TILE : (s + 1) * TILE] = jnp.broadcast_to(scale, (TILE, LANES))
                code = to_code(value, scale, top_code)
                if a == 0:
                    high = jnp.floor(code * (1.0 / BYTE))
                    lows.append(code - high * BYTE)
                    code = high
                code_to[a][q, :, lanes[s]] = narrow(code)
            for n in range(len(lows) // 2):
                code = lows[2 * n] * BYTE + (lows[2 * n + 1] - BYTE * BYTE / 2)
                code_to[a][q, :, width + n * LANES : width + (n + 1) * LANES] = narrow(code)

        def unpack(q):
            codes = [decode(code_from[a][q, :, lanes[s]]) for s in range(sides)]
            if a == 0:
                for n in range(sides // 2):
                    both = decode(code_from[a][q, :, width + n * LANES : width + (n + 1) * LANES])
                    both = both + BYTE * BYTE / 2
                    high = jnp.floor(both * (1.0 / BYTE))
                    codes[2 * n] = codes[2 * n] * BYTE + high
                    codes[2 * n + 1] = codes[2 * n + 1] * BYTE + (both - high * BYTE)
            for s in range(sides):
                scale = scale_from[a, q, s * TILE : s * TILE + 1] * (1.0 / top_code)
                image[:, lanes[s]] += codes[s] * scale

        @pl.loop(1, pairs + 2)
        def _(t):
            @pl.when(t <= pairs)
            def _():
                q = lax.rem(chip + t, pairs)
                to_partner[q] = far(2 * q + 1 - core)
                pair_copy(t - 1, q).start()

            @pl.when(t > 1)
            def _():
                i = t - 1
                q = lax.rem(chip + i, pairs)
                to_chips[q] = far(2 * q + core)
                pair_copy(i - 1, q).wait_recv()
                to_chips[q] = to_chips[q] + from_partner[q]

                @pl.when(i < pairs)
                def _():
                    pack(to_chips, q)
                    for copy in chip_copies(i - 1, q, chip):
                        copy.start()

        image[...] += to_chips[chip]
        for i in range(1, pairs):
            source = lax.rem(chip + pairs - i, pairs)
            for copy in chip_copies(i - 1, source, source):
                copy.wait_recv()
            unpack(source)
        for i in range(1, pairs + 1):
            q = lax.rem(chip + i, pairs)
            pair_copy(i - 1, q).wait_send()
            if i < pairs:
                for copy in chip_copies(i - 1, q, chip):
                    copy.wait_send()

    def slot_codes(value, scales, buffer):
        for s in range(0, sides, 2):
            codes = []
            for side in (s, s + 1):
                code = to_code(value[:, lanes[side]], scales[side], TOP)
                codes.append(split_dot(to_mesh, code, 2).reshape(count, capacity, LANES))
            both = jnp.concatenate(codes, axis=1)
            buffer[:, s * capacity : (s + 2) * capacity, :] = narrow(both)

    to_own = one_hot(
        turned_target[:, 0:1] * capacity + rank_column == iota((blocks, slots), 1)
    )
    to_source = one_hot(turned_target[:, 0:1] == iota((blocks, count), 1))

    def home(buffer, scales):
        values = []
        own_scales = split_dot(to_source, scales)
        for s in range(0, sides, 2):
            both = decode(buffer[:, s * capacity : (s + 2) * capacity, :])
            for side in (s, s + 1):
                code = both[:, (side - s) * capacity : (side - s + 1) * capacity]
                code = code.reshape(slots, LANES)
                high = code.astype(jnp.bfloat16)
                scale = own_scales[:, side : side + 1] * (1.0 / TOP)
                values.append(
                    (
                        split_dot(to_own, high, 1) * scale,
                        split_dot(to_own, code - high.astype(jnp.float32), 1) * scale,
                    )
                )
        return values

    operate(0, lambda: None)
    found = [[] for _ in range(7)]
    for s in range(sides):
        one, two = first_ref[:, lanes[s]], image[:, lanes[s]]
        along, size = total_of(one * two), total_of(one * one)
        guess = jnp.where(size > 1e-30, along / jnp.maximum(size, 1e-30), 0.0)
        rest = two - guess * one
        for place, value in enumerate(
            (
                along,
                guess,
                total_of(one * rest),
                total_of(rest * rest),
                size,
                largest(two),
                largest(one),
            )
        ):
            found[place].append(value)
    table = share(0, [value for values in found for value in values])()
    total = jnp.sum(table, axis=0, keepdims=True)
    projects, seconds, basis_scale = [], [], jnp.zeros((count, LANES), jnp.float32)
    for s in range(sides):
        guess, cross, rest, size, top_image, top_first = [
            table[:, n * sides + s : n * sides + s + 1] for n in range(1, 7)
        ]
        project = single(total, s) / panels
        off = guess - project
        norm = jnp.sqrt(
            jnp.sum(rest + off * (2.0 * cross + off * size), axis=0, keepdims=True) / panels
            + epsilon
        )
        value = (image[:, lanes[s]] - project * first_ref[:, lanes[s]]) / norm
        basis[:, lanes[s]] = value
        own[:, lanes[s]] = value.astype(jnp.bfloat16)
        bound = (top_image + jnp.abs(project) * top_first) / norm
        basis_scale = basis_scale + jnp.where(iota((count, LANES), 1) == s, bound, 0.0)
        projects.append(project)
        seconds.append(norm)
    mine_scale = jnp.sum(
        jnp.where(iota((count, LANES), 0) == me, basis_scale, 0.0), axis=0, keepdims=True
    )
    every = pl.ds(0, sides * capacity)
    basis_start, basis_recv, basis_send = to_all(1, sent_basis, landed_basis, every)
    image_start, image_recv, image_send = to_all(2, sent_image, landed_image, every)

    def send_basis():
        slot_codes(basis[...], [single(mine_scale, s) for s in range(sides)], sent_basis)
        basis_start()

    operate(1, send_basis)
    scales = [largest(image[:, lanes[s]]) for s in range(sides)]
    slot_codes(image[...], scales, sent_image)
    image_start()
    values = []
    for source in (first_ref, basis):
        for s in range(sides):
            values.append(total_of(source[:, lanes[s]] * image[:, lanes[s]]))
    wait = share(1, values + scales)
    basis_recv()
    returned = home(landed_basis, basis_scale)
    for s in range(sides):
        basis_ref[stride[s], :], basis_rest_ref[stride[s], :] = returned[s]
    table = wait()
    total = jnp.sum(table, axis=0, keepdims=True) / panels
    ends = [[single(total, n * sides + s) for s in range(sides)] for n in range(2)]
    for s in range(sides):
        line = jnp.zeros((1, LANES), jnp.float32)
        for place, found in enumerate((norms, projects, seconds, ends[0], ends[1])):
            line = line + jnp.where(lane_row == place, found[s], 0.0)
        entries_ref[s : s + 1] = line[:, : entries_ref.shape[1]]
    kept = iota((count, LANES), 1)
    image_scale = jnp.zeros((count, LANES), jnp.float32)
    for s in range(sides):
        image_scale = image_scale + jnp.where(
            kept == s, table[:, 2 * sides + s : 2 * sides + s + 1], 0.0
        )
    image_recv()
    landed_values = home(landed_image, image_scale)
    for s in range(sides):
        high, rest = landed_values[s]
        next_ref[stride[s], :] = high + rest - ends[0][s] * (side_ref[stride[s], :] / norms[s])
        next_rest_ref[stride[s], :] = ends[1][s] * (returned[s][0] + returned[s][1])
    basis_send()
    image_send()


def body(
    right_side,
    cluster_of,
    near_rows,
    near_columns,
    near_blocks,
    far_rows,
    far_columns,
    far_rank,
    far_left,
    far_right,
):
    rows = lax.axis_size("row")
    columns = lax.axis_size("col")
    count = rows * columns
    blocks, sides, lanes = right_side.shape
    width = sides * lanes
    capacity = max(TILE, 2 * blocks // count)
    near_groups = near_rows.shape[0] // lanes
    near_blocks = near_blocks.reshape(near_groups, -1, *near_blocks.shape[1:])
    far_left = far_left.reshape(columns, -1, *far_left.shape[1:])
    far_right = far_right.reshape(columns, -1, *far_right.shape[1:])
    near_count, far_count = near_blocks.shape[1], far_left.shape[1]
    halo = blocks // 4
    pairs = columns // 2
    dma = pltpu.SemaphoreType.DMA
    real, half, code = jnp.float32, jnp.bfloat16, jnp.int16
    out_slots = (count, sides * capacity + TILE, lanes)
    code_slots = (count, sides * capacity, lanes)
    hbm = pl.BlockSpec(memory_space=pl.ANY)
    basis, basis_rest, following, following_rest, entries = pl.pallas_call(
        functools.partial(arnoldi_kernel, rows, columns),
        out_shape=[
            *[jax.ShapeDtypeStruct((blocks * sides, lanes), real)] * 4,
            jax.ShapeDtypeStruct((sides, 5), real),
        ],
        in_specs=[VMEM] * 7 + [hbm] * 3,
        out_specs=[VMEM] * 5,
        scratch_shapes=[
            pltpu.VMEM((near_groups + columns, TILE, lanes), real),
            pltpu.VMEM((near_groups, near_count, blocks + 2 * halo), half),
            pltpu.VMEM((near_groups, blocks, near_count), half),
            pltpu.VMEM((near_groups, near_count, width), real),
            pltpu.VMEM((columns, far_count, rows * blocks), half),
            pltpu.VMEM((columns, blocks, far_count), half),
            pltpu.VMEM((columns, far_count, lanes), real),
            pltpu.VMEM((columns, far_count, width), half),
            pltpu.VMEM(out_slots, real),
            pltpu.VMEM(out_slots, real),
            pltpu.VMEM(code_slots, code),
            pltpu.VMEM(code_slots, code),
            pltpu.VMEM(code_slots, code),
            pltpu.VMEM(code_slots, code),
            pltpu.VMEM((blocks, width), real),
            pltpu.VMEM(near_blocks.shape, half),
            pltpu.VMEM(far_left.shape, half),
            pltpu.VMEM(far_right.shape, half),
            pltpu.VMEM((blocks, width), half),
            pltpu.VMEM((blocks, width), real),
            pltpu.VMEM((blocks, width), real),
            pltpu.VMEM((rows, blocks, width), half),
            pltpu.VMEM((blocks + 2 * halo, width), half),
            pltpu.VMEM((halo, width), half),
            pltpu.VMEM((halo, width), half),
            pltpu.VMEM((near_blocks.shape[1], width), real),
            pltpu.VMEM((far_left.shape[1], width), real),
            pltpu.VMEM((pairs, blocks, width), real),
            pltpu.VMEM((pairs, blocks, width), real),
            pltpu.VMEM((pairs, blocks, width), real),
            pltpu.VMEM((pairs, blocks, 3 * width // 2), code),
            pltpu.VMEM((pairs, blocks, 3 * width // 2), code),
            pltpu.VMEM((pairs, blocks, width), code),
            pltpu.VMEM((pairs, blocks, width), code),
            pltpu.VMEM((2, pairs, sides * TILE, lanes), real),
            pltpu.VMEM((2, pairs, sides * TILE, lanes), real),
            pltpu.VMEM((2, TILE, lanes), real),
            pltpu.VMEM((2, count, TILE, lanes), real),
            dma((3, max(columns, near_groups))),
            dma((2, 2)),
            dma((2, 2)),
            dma((2, 2, rows - 1)),
            dma((2, 2, rows - 1)),
            dma((2, pairs)),
            dma((2, pairs)),
            dma((2, pairs)),
            dma((2, pairs)),
            dma((2, pairs)),
            dma((2, pairs)),
            dma((5,)),
            dma((5,)),
        ],
        compiler_params=pltpu.CompilerParams(
            collective_id=0, has_side_effects=True, vmem_limit_bytes=LIMIT
        ),
    )(
        right_side.reshape(blocks * sides, lanes),
        cluster_of.reshape(1, blocks),
        near_columns.reshape(near_groups, -1),
        near_rows.reshape(near_groups, -1),
        far_columns.reshape(columns, -1),
        far_rows.reshape(columns, -1),
        far_rank.reshape(columns, -1),
        near_blocks,
        far_left,
        far_right,
    )
    shape = (blocks, sides, lanes)
    return (
        (basis + basis_rest).reshape(shape),
        (following - following_rest).reshape(shape),
        entries.T,
    )


def solution(mesh):
    vector = P(("row", "col"), None, None)
    table = P(("row", "col"))
    placed = (vector, table, table, table, vector, table, table, table, vector, vector)
    return jax.shard_map(
        body,
        mesh=mesh,
        in_specs=placed,
        out_specs=(vector, vector, P()),
        check_vma=False,
    )
```

```python
import functools

import jax
import jax.numpy as jnp
from jax import lax
from jax.experimental import pallas as pl
from jax.experimental.pallas import tpu as pltpu
from jax.sharding import PartitionSpec as P

epsilon = 1e-06
MESH = pl.DeviceIdType.MESH
VMEM = pl.BlockSpec(memory_space=pltpu.VMEM)
LANES = 128
LIMIT = 56 * 2**20
TILE = 8
TOP = 32767.0
WIDE = 8388607.0
BYTE = 256.0
HALVES = 2


def coordinates(index, column_count):
    return (lax.div(index, column_count), lax.rem(index, column_count))


def greet(me, rows, columns):
    count = rows * columns
    barrier = pltpu.get_barrier_semaphore()

    @pl.loop(1, count)
    def _(k):
        pl.semaphore_signal(
            barrier,
            inc=1,
            device_id=coordinates(lax.rem(me + k, count), columns),
            device_id_type=MESH,
        )

    return functools.partial(pl.semaphore_wait, barrier, count - 1)


def split_dot(picker, value, terms=3):
    parts = []
    for _ in range(terms):
        parts.append(value.astype(jnp.bfloat16))
        value = value - parts[-1].astype(jnp.float32)
    dot = functools.partial(jnp.dot, preferred_element_type=jnp.float32)
    if picker.shape[1] % LANES == 0:
        return dot(jnp.concatenate([picker] * terms, axis=1), jnp.concatenate(parts, axis=0))
    return sum(dot(picker, part) for part in parts)


def one_hot(condition):
    return jnp.where(condition, 1.0, 0.0).astype(jnp.bfloat16)


def remote(source, destination, sends, recvs, k, device):
    return pltpu.make_async_remote_copy(
        src_ref=source,
        dst_ref=destination,
        send_sem=sends.at[k],
        recv_sem=recvs.at[k],
        device_id=device,
        device_id_type=MESH,
    )


def corners(one, two):
    empty = jnp.zeros_like(one)
    return jnp.concatenate(
        [jnp.concatenate([one, empty], axis=1), jnp.concatenate([empty, two], axis=1)], axis=0
    )


def near_group(sides, g, near_picked, near_place, near_ref, near_out, image, terms):
    near_count = near_ref.shape[1]
    half = 8
    both = 2 * half
    shape = (sides * half, LANES)
    row_id = lax.rem(lax.broadcasted_iota(jnp.int32, shape, 0), half)
    for j in range(near_count // both):
        here = [slice(j * both + n * half, j * both + (n + 1) * half) for n in range(2)]
        rows = [
            jnp.concatenate(
                [near_picked[g, here[n], s * LANES : (s + 1) * LANES] for s in range(sides)],
                axis=0,
            ).astype(jnp.bfloat16)
            for n in range(2)
        ]
        weights = jnp.concatenate(
            [near_ref[g, here[n]].reshape(half * LANES, LANES) for n in range(2)], axis=1
        )
        product = lax.dot_general(
            corners(*rows), weights, (((1,), (1,)), ((), ())), preferred_element_type=jnp.float32
        )
        for n in range(2):
            part = product[n * sides * half : (n + 1) * sides * half]
            value = part[:, :LANES]
            for e in range(1, half):
                value = jnp.where(row_id == e, part[:, e * LANES : (e + 1) * LANES], value)
            for s in range(sides):
                near_out[here[n], s * LANES : (s + 1) * LANES] = value[s * half : (s + 1) * half]
    image[...] += split_dot(near_place[g], near_out[...], terms)


def far_group(
    sides, terms, chosen, far_picked, far_place, far_ranks, far_left, far_right, far_out
):
    far_count, rank = far_left.shape[1:3]
    half = 16
    both = 2 * half
    shape = (sides * half, half * rank)
    entry = lax.rem(lax.broadcasted_iota(jnp.int32, shape, 0), half)
    lane = lax.broadcasted_iota(jnp.int32, shape, 1)
    term = lax.rem(lane, rank).astype(jnp.float32)
    own_entry = lax.div(lane, rank) == entry
    kept = []
    batches = [
        (n, g, [slice(j * both + m * half, j * both + (m + 1) * half) for m in range(2)])
        for n, g in enumerate(chosen)
        for j in range(far_count // both)
    ]

    def weights(factor, g, here):
        return jnp.concatenate(
            [factor[g, part].reshape(half * rank, LANES) for part in here], axis=1
        )

    for _, g, here in batches:
        rows = [
            jnp.concatenate(
                [far_picked[g, part, s * LANES : (s + 1) * LANES] for s in range(sides)], axis=0
            )
            for part in here
        ]
        product = lax.dot_general(
            corners(*rows),
            weights(far_right, g, here),
            (((1,), (1,)), ((), ())),
            preferred_element_type=jnp.float32,
        )
        parts = []
        for m in range(2):
            ranks = jnp.concatenate([far_ranks[g, here[m], 0:1]] * sides, axis=0)
            part = product[m * sides * half : (m + 1) * sides * half]
            parts.append(jnp.where(own_entry & (term < ranks), part, 0.0).astype(jnp.bfloat16))
        kept.append(jnp.concatenate(parts, axis=0))
    for (n, g, here), coefficients in zip(batches, kept):
        value = jnp.dot(
            coefficients, weights(far_left, g, here), preferred_element_type=jnp.float32
        )
        for m in range(2):
            part = value[m * sides * half : (m + 1) * sides * half, m * LANES : (m + 1) * LANES]
            for s in range(sides):
                far_out[n, here[m], s * LANES : (s + 1) * LANES] = part[s * half : (s + 1) * half]
    return [split_dot(far_place[g], far_out[n], terms) for n, g in enumerate(chosen)]


def iota(shape, dimension):
    return lax.broadcasted_iota(jnp.int32, shape, dimension)


def to_code(value, scale, top):
    return jnp.floor(jnp.clip(value * (top / scale), -top, top) + 0.5)


def narrow(code):
    return code.astype(jnp.int32).astype(jnp.int16)


def decode(code):
    return code.astype(jnp.int32).astype(jnp.float32)


def largest(value):
    top = jnp.max(jnp.abs(value), axis=0, keepdims=True)
    return jnp.maximum(jnp.max(top, axis=1, keepdims=True), 1e-30)


def total_of(value):
    return jnp.sum(jnp.sum(value, axis=0, keepdims=True), axis=1, keepdims=True)


def arnoldi_kernel(
    rows,
    columns,
    side_ref,
    cluster_ref,
    near_columns_ref,
    near_rows_ref,
    far_columns_ref,
    far_rows_ref,
    far_rank_ref,
    near_hbm,
    far_left_hbm,
    far_right_hbm,
    basis_ref,
    basis_rest_ref,
    next_ref,
    next_rest_ref,
    entries_ref,
    tables,
    near_pick,
    near_place,
    near_picked,
    far_pick,
    far_place,
    far_ranks,
    far_picked,
    sent,
    landed,
    sent_basis,
    landed_basis,
    sent_image,
    landed_image,
    first_ref,
    near_ref,
    far_left,
    far_right,
    own,
    basis,
    image,
    everything,
    extended,
    left,
    right,
    near_out,
    far_out,
    to_partner,
    from_partner,
    to_chips,
    wide_to,
    wide_from,
    code_to,
    code_from,
    scale_to,
    scale_from,
    mine,
    parts,
    load_sem,
    halo_send,
    halo_recv,
    spread_send,
    spread_recv,
    pair_send,
    pair_recv,
    chip_send,
    chip_recv,
    scale_send,
    scale_recv,
    all_send,
    all_recv,
):
    row, column = lax.axis_index("row"), lax.axis_index("col")
    count = rows * columns
    me = row * columns + column
    blocks, width = first_ref.shape
    sides = width // LANES
    halo = left.shape[1]
    groups = far_left.shape[0]
    near_groups = near_ref.shape[0]
    pairs = columns // 2
    chip, core = lax.div(column, 2), lax.rem(column, 2)
    partner = 2 * chip + 1 - core
    panels = count * blocks * LANES
    lanes = [slice(s * LANES, (s + 1) * LANES) for s in range(sides)]
    capacity = (sent.shape[1] - TILE) // sides
    slots = count * capacity
    lane_row = iota((1, LANES), 1)
    some = sides // HALVES
    code_to, code_from = (wide_to, code_to), (wide_from, code_from)
    entered = greet(me, rows, columns)

    def load(kind, g):
        source, target = (
            (near_hbm, near_ref),
            (far_left_hbm, far_left),
            (far_right_hbm, far_right),
        )[kind]
        return pltpu.make_async_copy(source.at[g], target.at[g], load_sem.at[kind, g])

    for kind, many in enumerate((near_groups, groups, groups)):

        @pl.loop(0, many)
        def _(g, kind=kind):
            load(kind, g).start()

    def to_all(n, source, destination, part):
        def copy(peer, there, here):
            return pltpu.make_async_remote_copy(
                src_ref=source.at[there, part],
                dst_ref=destination.at[here, part],
                send_sem=all_send.at[n],
                recv_sem=all_recv.at[n],
                device_id=coordinates(peer, columns),
                device_id_type=MESH,
            )

        def start():
            @pl.loop(1, count)
            def _(k):
                peer = lax.rem(me + k, count)
                copy(peer, peer, me).start()

            destination[me] = source[me]

        every = copy(lax.rem(me + 1, count), pl.ds(0, count - 1), pl.ds(0, count - 1))
        return start, every.wait_recv, every.wait_send

    def share(n, values):
        row_of = jnp.zeros((1, LANES), jnp.float32)
        for place, value in enumerate(values):
            row_of = row_of + jnp.where(lane_row == place, value, 0.0)
        mine[n] = jnp.broadcast_to(row_of, (TILE, LANES))

        def copy(peer, here):
            return pltpu.make_async_remote_copy(
                src_ref=(
                    parts.at[n, pl.ds(0, count - 1), pl.ds(0, 1)]
                    if here is None
                    else mine.at[n, pl.ds(0, 1)]
                ),
                dst_ref=parts.at[n, pl.ds(0, count - 1) if here is None else here, pl.ds(0, 1)],
                send_sem=all_send.at[3 + n],
                recv_sem=all_recv.at[3 + n],
                device_id=coordinates(peer, columns),
                device_id_type=MESH,
            )

        @pl.loop(1, count)
        def _(k):
            copy(lax.rem(me + k, count), me).start()

        parts[n, me] = mine[n]
        every = copy(lax.rem(me + 1, count), None)

        def wait():
            every.wait_recv()
            every.wait_send()
            return parts[n, :, 0, :]

        return wait

    def single(total, place):
        return jnp.sum(jnp.where(lane_row == place, total, 0.0), axis=1, keepdims=True)

    cluster = cluster_ref[...]
    target = lax.div(cluster, blocks)
    turned = jnp.broadcast_to(cluster.astype(jnp.float32), (blocks, blocks)).T.astype(jnp.int32)
    turned_target = lax.div(turned, blocks)
    place = turned - turned_target * blocks
    square = (blocks, blocks)
    same = turned_target == target
    ranks = jnp.where(same & (iota(square, 1) < iota(square, 0)), 1, 0)
    rank_column = jnp.sum(ranks, axis=1, keepdims=True)
    ranks = jnp.where(same & (iota(square, 0) < iota(square, 1)), 1, 0)
    rank_row = jnp.sum(ranks, axis=0, keepdims=True)
    slot_shape = (slots, blocks)
    to_slot = one_hot(iota(slot_shape, 0) == target * capacity + rank_row)
    to_device = one_hot(lax.div(iota(slot_shape, 0), capacity) == target)
    marks = jnp.where(iota(square, 1) == rank_column, place + 1, 0)
    extra = jnp.dot(
        to_device,
        marks.astype(jnp.float32).astype(jnp.bfloat16),
        preferred_element_type=jnp.float32,
    )
    stride = [pl.ds(s, blocks, stride=sides) for s in range(sides)]
    for s in range(sides):
        value = side_ref[stride[s], :]
        extra = extra + jnp.where(lane_row == capacity + s, total_of(value * value), 0.0)
        picked = split_dot(to_slot, value)
        sent[:, s * capacity : (s + 1) * capacity, :] = picked.reshape(count, capacity, LANES)
    top = sides * capacity
    if capacity == TILE:
        sent[:, top:, :] = extra.reshape(count, TILE, LANES)
    else:
        sent[:, top:, :] = extra.reshape(count, capacity, LANES)[:, :TILE]
    entered()
    out_start, out_recv, out_send = to_all(0, sent, landed, pl.ds(0, top + 1))
    out_start()

    near_count, far_count = near_ref.shape[1], far_left.shape[1]

    def turn(g, *sources):
        tables[g] = jnp.zeros(tables.shape[1:], jnp.float32)
        for spot, source in enumerate(sources):
            tables[g, spot : spot + 1, : source.shape[1]] = source.astype(jnp.float32)
        return tables[g].T

    def matches(column, many):
        return one_hot(column == iota((column.shape[0], many), 1).astype(jnp.float32))

    def places(row_of):
        return one_hot(iota((blocks, row_of.shape[1]), 0) == row_of)

    for g in range(near_groups):
        column_of = turn(g, near_columns_ref[g : g + 1])
        near_pick[g] = matches(column_of[:near_count, 0:1], extended.shape[0])
        near_place[g] = places(near_rows_ref[g : g + 1])
    for g in range(groups):
        column_of = turn(near_groups + g, far_columns_ref[g : g + 1], far_rank_ref[g : g + 1])
        far_pick[g] = matches(column_of[:far_count, 0:1], rows * blocks)
        far_ranks[g] = jnp.broadcast_to(column_of[:far_count, 1:2], far_ranks.shape[1:])
        far_place[g] = places(far_rows_ref[g : g + 1] - g * blocks)

    out_recv()
    table = landed[:, top, :]
    total = jnp.sum(table, axis=0, keepdims=True)
    norms = [
        jnp.sqrt(single(total, capacity + s) / panels + epsilon) for s in range(sides)
    ]
    spread_marks = jnp.dot(
        one_hot(lax.div(iota((slots, count), 0), capacity) == iota((slots, count), 1)),
        jnp.where(iota((count, LANES), 1) < capacity, table, 0.0).astype(jnp.bfloat16),
        preferred_element_type=jnp.float32,
    )
    wide = (slots, LANES)
    held = jnp.sum(
        jnp.where(lax.rem(iota(wide, 0), capacity) == iota(wide, 1), spread_marks, 0.0),
        axis=1,
        keepdims=True,
    ).astype(jnp.int32) - 1
    to_mesh_wide = jnp.where(held == iota((slots, blocks), 1), 1.0, 0.0)
    to_mesh = to_mesh_wide.astype(jnp.bfloat16)
    to_cluster = to_mesh_wide.T.astype(jnp.bfloat16)
    for s in range(sides):
        arrived = landed[:, s * capacity : (s + 1) * capacity, :].reshape(slots, LANES)
        value = split_dot(to_cluster, arrived) / norms[s]
        first_ref[:, lanes[s]] = value
        own[s // some, :, lanes[s % some]] = value.astype(jnp.bfloat16)
    out_send()

    part_width = width // HALVES
    parts_of = [slice(h * part_width, (h + 1) * part_width) for h in range(HALVES)]

    def operate(a, prepare, between):
        after = coordinates(lax.rem(me + 1, count), columns)
        before = coordinates(lax.rem(me + count - 1, count), columns)
        halos = [
            remote(
                own.at[:, pl.ds(blocks - halo, halo)],
                left,
                halo_send.at[a],
                halo_recv.at[a],
                0,
                after,
            ),
            remote(own.at[:, pl.ds(0, halo)], right, halo_send.at[a], halo_recv.at[a], 1, before),
        ]
        for copy in halos:
            copy.start()
        for h in range(HALVES):
            everything[h, row] = own[h]

        def inside(index):
            return (index >= 0) & (index < rows)

        def hop(h, way, distance, source):
            sign = 1 - 2 * way
            reach = 2 if distance == 2 else 1
            return remote(
                everything.at[h, source],
                everything.at[h, source],
                spread_send.at[a, h, way],
                spread_recv.at[a, h, way],
                distance - 1,
                (lax.rem(row + sign * reach + 2 * rows, rows), column),
            )

        def arrive(h, distance):
            for way in range(2):
                source = row - (1 - 2 * way) * distance

                @pl.when(inside(source))
                def _(way=way, source=source):
                    hop(h, way, distance, source).wait_recv()

        def each_hop(h, distance, act):
            for way in range(2):
                sign = 1 - 2 * way
                held_at = 0 if distance < 3 else distance - 1
                source = row - sign * held_at
                there = row + sign * (2 if distance == 2 else 1)

                @pl.when(inside(source) & inside(there))
                def _(way=way, source=source):
                    act(hop(h, way, distance, source))

        def begin(copy):
            copy.start()

        for h in range(HALVES):
            for distance in range(1, min(rows, 3)):
                each_hop(h, distance, begin)
        image[...] = 0.5 * basis_or_first[a][...].astype(jnp.bfloat16).astype(jnp.float32)
        for h in range(HALVES):
            extended[halo : halo + blocks, parts_of[h]] = own[h]
        for copy in halos:
            copy.wait()
        for h in range(HALVES):
            extended[0:halo, parts_of[h]] = left[h]
            extended[halo + blocks :, parts_of[h]] = right[h]
        for g in range(near_groups):
            near_picked[g] = jnp.dot(
                near_pick[g], extended[...], preferred_element_type=jnp.float32
            )
        relays = [(h, distance) for distance in range(3, rows) for h in range(HALVES)]

        def relay(h, distance):
            arrive(h, distance - 1)
            each_hop(h, distance, begin)

        early = min(len(relays), near_groups - 1)

        @pl.loop(0, near_groups)
        def _(g):
            if a == 0:
                load(0, g).wait()
            near_group(sides, g, near_picked, near_place, near_ref, near_out, image, 3 - a)
            for n in range(early):

                @pl.when(g == near_groups - early + n)
                def _(n=n):
                    relay(*relays[n])

        for step in relays[early:]:
            relay(*step)
        prepare()
        if a == 0:
            for kind in (1, 2):

                @pl.loop(0, groups)
                def _(g, kind=kind):
                    load(kind, g).wait()

        far = functools.partial(
            far_group,
            some,
            3 - a,
            far_place=far_place,
            far_ranks=far_ranks,
            far_left=far_left,
            far_right=far_right,
            far_out=far_out,
        )

        def pair_copy(h, k, q):
            return remote(
                to_partner.at[h, q],
                from_partner.at[h, q],
                pair_send.at[a, h],
                pair_recv.at[a, h],
                k,
                (row, partner),
            )

        def chip_copies(h, k, q, here):
            device = (row, 2 * q + core)
            return [
                remote(
                    code_to[a].at[h, q],
                    code_from[a].at[h, here],
                    chip_send.at[a, h],
                    chip_recv.at[a, h],
                    k,
                    device,
                ),
                remote(
                    scale_to.at[a, h, q],
                    scale_from.at[a, h, here],
                    scale_send.at[a, h],
                    scale_recv.at[a, h],
                    k,
                    device,
                ),
            ]

        top_code = WIDE if a == 0 else TOP

        def pack(h, q):
            lows = []
            for s in range(some):
                value = to_chips[h, q, :, lanes[s]]
                scale = jnp.maximum(jnp.max(jnp.abs(value), axis=0, keepdims=True), 1e-30)
                scale_to[a, h, q, s * TILE : (s + 1) * TILE] = jnp.broadcast_to(
                    scale, (TILE, LANES)
                )
                code = to_code(value, scale, top_code)
                if a == 0:
                    high = jnp.floor(code * (1.0 / BYTE))
                    lows.append(code - high * BYTE)
                    code = high
                code_to[a][h, q, :, lanes[s]] = narrow(code)
            for n in range(len(lows) // 2):
                code = lows[2 * n] * BYTE + (lows[2 * n + 1] - BYTE * BYTE / 2)
                code_to[a][h, q, :, lanes[some + n]] = narrow(code)

        def unpack(h, q):
            codes = [decode(code_from[a][h, q, :, lanes[s]]) for s in range(some)]
            if a == 0:
                for n in range(some // 2):
                    both = decode(code_from[a][h, q, :, lanes[some + n]])
                    both = both + BYTE * BYTE / 2
                    high = jnp.floor(both * (1.0 / BYTE))
                    codes[2 * n] = codes[2 * n] * BYTE + high
                    codes[2 * n + 1] = codes[2 * n + 1] * BYTE + (both - high * BYTE)
            for s in range(some):
                scale = scale_from[a, h, q, s * TILE : s * TILE + 1] * (1.0 / top_code)
                image[:, lanes[h * some + s]] += codes[s] * scale

        for h in range(HALVES):
            for distance in sorted({1, rows - 1}):
                arrive(h, distance)
            for g in range(groups):
                far_picked[h, g] = jnp.dot(
                    far_pick[g],
                    everything[h].reshape(rows * blocks, part_width),
                    preferred_element_type=jnp.float32,
                ).astype(jnp.bfloat16)

            @pl.loop(1, pairs + 2)
            def _(t, h=h):
                @pl.when(t <= pairs)
                def _():
                    q = lax.rem(chip + t, pairs)
                    to_partner[h, q], to_chips[h, q] = far(
                        [2 * q + 1 - core, 2 * q + core], far_picked=far_picked.at[h]
                    )
                    pair_copy(h, t - 1, q).start()

                @pl.when(t > 1)
                def _():
                    i = t - 1
                    q = lax.rem(chip + i, pairs)
                    pair_copy(h, i - 1, q).wait_recv()
                    to_chips[h, q] = to_chips[h, q] + from_partner[h, q]

                    @pl.when(i < pairs)
                    def _():
                        pack(h, q)
                        for copy in chip_copies(h, i - 1, q, chip):
                            copy.start()

            if h == HALVES - 1:
                between()
        for h in range(HALVES):
            image[:, parts_of[h]] += to_chips[h, chip]
            for i in range(1, pairs):
                source = lax.rem(chip + pairs - i, pairs)
                for copy in chip_copies(h, i - 1, source, source):
                    copy.wait_recv()
                unpack(h, source)
        for h in range(HALVES):
            for distance in range(1, rows):
                each_hop(h, distance, lambda copy: copy.wait_send())
            for i in range(1, pairs + 1):
                q = lax.rem(chip + i, pairs)
                pair_copy(h, i - 1, q).wait_send()
                if i < pairs:
                    for copy in chip_copies(h, i - 1, q, chip):
                        copy.wait_send()

    basis_or_first = (first_ref, basis)

    def slot_codes(value, scales, buffer):
        for s in range(0, sides, 2):
            codes = []
            for side in (s, s + 1):
                code = to_code(value[:, lanes[side]], scales[side], TOP)
                codes.append(split_dot(to_mesh, code, 2).reshape(count, capacity, LANES))
            both = jnp.concatenate(codes, axis=1)
            buffer[:, s * capacity : (s + 2) * capacity, :] = narrow(both)

    to_own = one_hot(
        turned_target[:, 0:1] * capacity + rank_column == iota((blocks, slots), 1)
    )
    to_source = one_hot(turned_target[:, 0:1] == iota((blocks, count), 1))

    def home(buffer, scales):
        values = []
        own_scales = split_dot(to_source, scales)
        for s in range(0, sides, 2):
            both = decode(buffer[:, s * capacity : (s + 2) * capacity, :])
            for side in (s, s + 1):
                code = both[:, (side - s) * capacity : (side - s + 1) * capacity]
                code = code.reshape(slots, LANES)
                high = code.astype(jnp.bfloat16)
                scale = own_scales[:, side : side + 1] * (1.0 / TOP)
                values.append(
                    (
                        split_dot(to_own, high, 1) * scale,
                        split_dot(to_own, code - high.astype(jnp.float32), 1) * scale,
                    )
                )
        return values

    operate(0, lambda: None, lambda: None)
    found = [[] for _ in range(7)]
    for s in range(sides):
        one, two = first_ref[:, lanes[s]], image[:, lanes[s]]
        along, size = total_of(one * two), total_of(one * one)
        guess = jnp.where(size > 1e-30, along / jnp.maximum(size, 1e-30), 0.0)
        rest = two - guess * one
        for place, value in enumerate(
            (
                along,
                guess,
                total_of(one * rest),
                total_of(rest * rest),
                size,
                largest(two),
                largest(one),
            )
        ):
            found[place].append(value)
    table = share(0, [value for values in found for value in values])()
    total = jnp.sum(table, axis=0, keepdims=True)
    projects, seconds, basis_scale = [], [], jnp.zeros((count, LANES), jnp.float32)
    for s in range(sides):
        guess, cross, rest, size, top_image, top_first = [
            table[:, n * sides + s : n * sides + s + 1] for n in range(1, 7)
        ]
        project = single(total, s) / panels
        off = guess - project
        norm = jnp.sqrt(
            jnp.sum(rest + off * (2.0 * cross + off * size), axis=0, keepdims=True) / panels
            + epsilon
        )
        value = (image[:, lanes[s]] - project * first_ref[:, lanes[s]]) / norm
        basis[:, lanes[s]] = value
        own[s // some, :, lanes[s % some]] = value.astype(jnp.bfloat16)
        bound = (top_image + jnp.abs(project) * top_first) / norm
        basis_scale = basis_scale + jnp.where(iota((count, LANES), 1) == s, bound, 0.0)
        projects.append(project)
        seconds.append(norm)
    mine_scale = jnp.sum(
        jnp.where(iota((count, LANES), 0) == me, basis_scale, 0.0), axis=0, keepdims=True
    )
    every = pl.ds(0, sides * capacity)
    basis_start, basis_recv, basis_send = to_all(1, sent_basis, landed_basis, every)
    image_start, image_recv, image_send = to_all(2, sent_image, landed_image, every)

    def code_basis():
        slot_codes(basis[...], [single(mine_scale, s) for s in range(sides)], sent_basis)

    operate(1, code_basis, basis_start)
    scales = [largest(image[:, lanes[s]]) for s in range(sides)]
    slot_codes(image[...], scales, sent_image)
    image_start()
    values = []
    for source in (first_ref, basis):
        for s in range(sides):
            values.append(total_of(source[:, lanes[s]] * image[:, lanes[s]]))
    wait = share(1, values + scales)
    basis_recv()
    returned = home(landed_basis, basis_scale)
    for s in range(sides):
        basis_ref[stride[s], :], basis_rest_ref[stride[s], :] = returned[s]
    table = wait()
    total = jnp.sum(table, axis=0, keepdims=True) / panels
    ends = [[single(total, n * sides + s) for s in range(sides)] for n in range(2)]
    for s in range(sides):
        line = jnp.zeros((1, LANES), jnp.float32)
        for place, found in enumerate((norms, projects, seconds, ends[0], ends[1])):
            line = line + jnp.where(lane_row == place, found[s], 0.0)
        entries_ref[s : s + 1] = line[:, : entries_ref.shape[1]]
    kept = iota((count, LANES), 1)
    image_scale = jnp.zeros((count, LANES), jnp.float32)
    for s in range(sides):
        image_scale = image_scale + jnp.where(
            kept == s, table[:, 2 * sides + s : 2 * sides + s + 1], 0.0
        )
    image_recv()
    landed_values = home(landed_image, image_scale)
    for s in range(sides):
        high, rest = landed_values[s]
        next_ref[stride[s], :] = high + rest - ends[0][s] * (side_ref[stride[s], :] / norms[s])
        next_rest_ref[stride[s], :] = ends[1][s] * (returned[s][0] + returned[s][1])
    basis_send()
    image_send()


def body(
    right_side,
    cluster_of,
    near_rows,
    near_columns,
    near_blocks,
    far_rows,
    far_columns,
    far_rank,
    far_left,
    far_right,
):
    rows = lax.axis_size("row")
    columns = lax.axis_size("col")
    count = rows * columns
    blocks, sides, lanes = right_side.shape
    width = sides * lanes
    capacity = max(TILE, 2 * blocks // count)
    near_groups = near_rows.shape[0] // lanes
    near_blocks = near_blocks.reshape(near_groups, -1, *near_blocks.shape[1:])
    far_left = far_left.reshape(columns, -1, *far_left.shape[1:])
    far_right = far_right.reshape(columns, -1, *far_right.shape[1:])
    near_count, far_count = near_blocks.shape[1], far_left.shape[1]
    halo = blocks // 4
    pairs = columns // 2
    part = width // HALVES
    dma = pltpu.SemaphoreType.DMA
    real, half, code = jnp.float32, jnp.bfloat16, jnp.int16
    out_slots = (count, sides * capacity + TILE, lanes)
    code_slots = (count, sides * capacity, lanes)
    hbm = pl.BlockSpec(memory_space=pl.ANY)
    basis, basis_rest, following, following_rest, entries = pl.pallas_call(
        functools.partial(arnoldi_kernel, rows, columns),
        out_shape=[
            *[jax.ShapeDtypeStruct((blocks * sides, lanes), real)] * 4,
            jax.ShapeDtypeStruct((sides, 5), real),
        ],
        in_specs=[VMEM] * 7 + [hbm] * 3,
        out_specs=[VMEM] * 5,
        scratch_shapes=[
            pltpu.VMEM((near_groups + columns, TILE, lanes), real),
            pltpu.VMEM((near_groups, near_count, blocks + 2 * halo), half),
            pltpu.VMEM((near_groups, blocks, near_count), half),
            pltpu.VMEM((near_groups, near_count, width), real),
            pltpu.VMEM((columns, far_count, rows * blocks), half),
            pltpu.VMEM((columns, blocks, far_count), half),
            pltpu.VMEM((columns, far_count, lanes), real),
            pltpu.VMEM((HALVES, columns, far_count, part), half),
            pltpu.VMEM(out_slots, real),
            pltpu.VMEM(out_slots, real),
            pltpu.VMEM(code_slots, code),
            pltpu.VMEM(code_slots, code),
            pltpu.VMEM(code_slots, code),
            pltpu.VMEM(code_slots, code),
            pltpu.VMEM((blocks, width), real),
            pltpu.VMEM(near_blocks.shape, half),
            pltpu.VMEM(far_left.shape, half),
            pltpu.VMEM(far_right.shape, half),
            pltpu.VMEM((HALVES, blocks, part), half),
            pltpu.VMEM((blocks, width), real),
            pltpu.VMEM((blocks, width), real),
            pltpu.VMEM((HALVES, rows, blocks, part), half),
            pltpu.VMEM((blocks + 2 * halo, width), half),
            pltpu.VMEM((HALVES, halo, part), half),
            pltpu.VMEM((HALVES, halo, part), half),
            pltpu.VMEM((near_count, width), real),
            pltpu.VMEM((2, far_count, part), real),
            pltpu.VMEM((HALVES, pairs, blocks, part), real),
            pltpu.VMEM((HALVES, pairs, blocks, part), real),
            pltpu.VMEM((HALVES, pairs, blocks, part), real),
            pltpu.VMEM((HALVES, pairs, blocks, 3 * part // 2), code),
            pltpu.VMEM((HALVES, pairs, blocks, 3 * part // 2), code),
            pltpu.VMEM((HALVES, pairs, blocks, part), code),
            pltpu.VMEM((HALVES, pairs, blocks, part), code),
            pltpu.VMEM((2, HALVES, pairs, sides // HALVES * TILE, lanes), real),
            pltpu.VMEM((2, HALVES, pairs, sides // HALVES * TILE, lanes), real),
            pltpu.VMEM((2, TILE, lanes), real),
            pltpu.VMEM((2, count, TILE, lanes), real),
            dma((3, max(columns, near_groups))),
            dma((2, 2)),
            dma((2, 2)),
            dma((2, HALVES, 2, rows - 1)),
            dma((2, HALVES, 2, rows - 1)),
            dma((2, HALVES, pairs)),
            dma((2, HALVES, pairs)),
            dma((2, HALVES, pairs)),
            dma((2, HALVES, pairs)),
            dma((2, HALVES, pairs)),
            dma((2, HALVES, pairs)),
            dma((5,)),
            dma((5,)),
        ],
        compiler_params=pltpu.CompilerParams(
            collective_id=0, has_side_effects=True, vmem_limit_bytes=LIMIT
        ),
    )(
        right_side.reshape(blocks * sides, lanes),
        cluster_of.reshape(1, blocks),
        near_columns.reshape(near_groups, -1),
        near_rows.reshape(near_groups, -1),
        far_columns.reshape(columns, -1),
        far_rows.reshape(columns, -1),
        far_rank.reshape(columns, -1),
        near_blocks,
        far_left,
        far_right,
    )
    shape = (blocks, sides, lanes)
    return (
        (basis + basis_rest).reshape(shape),
        (following - following_rest).reshape(shape),
        entries.T,
    )


def solution(mesh):
    vector = P(("row", "col"), None, None)
    table = P(("row", "col"))
    placed = (vector, table, table, table, vector, table, table, table, vector, vector)
    return jax.shard_map(
        body,
        mesh=mesh,
        in_specs=placed,
        out_specs=(vector, vector, P()),
        check_vma=False,
    )
```

```python
import functools

import jax
import jax.numpy as jnp
from jax import lax
from jax.experimental import pallas as pl
from jax.experimental.pallas import tpu as pltpu
from jax.sharding import PartitionSpec as P

epsilon = 1e-06
MESH = pl.DeviceIdType.MESH
VMEM = pl.BlockSpec(memory_space=pltpu.VMEM)
LANES = 128
LIMIT = 56 * 2**20
TILE = 8
TOP = 32767.0
WIDE = 8388607.0
BYTE = 256.0
HALVES = 2


def coordinates(index, column_count):
    return (lax.div(index, column_count), lax.rem(index, column_count))


def greet(me, rows, columns):
    count = rows * columns
    barrier = pltpu.get_barrier_semaphore()

    @pl.loop(1, count)
    def _(k):
        pl.semaphore_signal(
            barrier,
            inc=1,
            device_id=coordinates(lax.rem(me + k, count), columns),
            device_id_type=MESH,
        )

    return functools.partial(pl.semaphore_wait, barrier, count - 1)


def split_dot(picker, value, terms=3):
    parts = []
    for _ in range(terms):
        parts.append(value.astype(jnp.bfloat16))
        value = value - parts[-1].astype(jnp.float32)
    dot = functools.partial(jnp.dot, preferred_element_type=jnp.float32)
    if picker.shape[1] % LANES == 0:
        return dot(jnp.concatenate([picker] * terms, axis=1), jnp.concatenate(parts, axis=0))
    return sum(dot(picker, part) for part in parts)


def one_hot(condition):
    return jnp.where(condition, 1.0, 0.0).astype(jnp.bfloat16)


def remote(source, destination, sends, recvs, k, device):
    return pltpu.make_async_remote_copy(
        src_ref=source,
        dst_ref=destination,
        send_sem=sends.at[k],
        recv_sem=recvs.at[k],
        device_id=device,
        device_id_type=MESH,
    )


def corners(one, two):
    empty = jnp.zeros_like(one)
    return jnp.concatenate(
        [jnp.concatenate([one, empty], axis=1), jnp.concatenate([empty, two], axis=1)], axis=0
    )


def near_group(sides, g, near_picked, near_place, near_ref, near_out, image, terms):
    near_count = near_ref.shape[1]
    half = 8
    both = 2 * half
    shape = (sides * half, LANES)
    row_id = lax.rem(lax.broadcasted_iota(jnp.int32, shape, 0), half)
    for j in range(near_count // both):
        here = [slice(j * both + n * half, j * both + (n + 1) * half) for n in range(2)]
        rows = [
            jnp.concatenate(
                [near_picked[g, here[n], s * LANES : (s + 1) * LANES] for s in range(sides)],
                axis=0,
            ).astype(jnp.bfloat16)
            for n in range(2)
        ]
        weights = jnp.concatenate(
            [near_ref[g, here[n]].reshape(half * LANES, LANES) for n in range(2)], axis=1
        )
        product = lax.dot_general(
            corners(*rows), weights, (((1,), (1,)), ((), ())), preferred_element_type=jnp.float32
        )
        for n in range(2):
            part = product[n * sides * half : (n + 1) * sides * half]
            value = part[:, :LANES]
            for e in range(1, half):
                value = jnp.where(row_id == e, part[:, e * LANES : (e + 1) * LANES], value)
            for s in range(sides):
                near_out[here[n], s * LANES : (s + 1) * LANES] = value[s * half : (s + 1) * half]
    image[...] += split_dot(near_place[g], near_out[...], terms)


def far_group(
    sides, terms, chosen, far_picked, far_place, far_ranks, far_left, far_right, far_out
):
    far_count, rank = far_left.shape[1:3]
    half = 16
    both = 2 * half
    shape = (sides * half, half * rank)
    entry = lax.rem(lax.broadcasted_iota(jnp.int32, shape, 0), half)
    lane = lax.broadcasted_iota(jnp.int32, shape, 1)
    term = lax.rem(lane, rank).astype(jnp.float32)
    own_entry = lax.div(lane, rank) == entry
    kept = []
    batches = [
        (n, g, [slice(j * both + m * half, j * both + (m + 1) * half) for m in range(2)])
        for n, g in enumerate(chosen)
        for j in range(far_count // both)
    ]

    def weights(factor, g, here):
        return jnp.concatenate(
            [factor[g, part].reshape(half * rank, LANES) for part in here], axis=1
        )

    for _, g, here in batches:
        rows = [
            jnp.concatenate(
                [far_picked[g, part, s * LANES : (s + 1) * LANES] for s in range(sides)], axis=0
            )
            for part in here
        ]
        product = lax.dot_general(
            corners(*rows),
            weights(far_right, g, here),
            (((1,), (1,)), ((), ())),
            preferred_element_type=jnp.float32,
        )
        parts = []
        for m in range(2):
            ranks = jnp.concatenate([far_ranks[g, here[m], 0:1]] * sides, axis=0)
            part = product[m * sides * half : (m + 1) * sides * half]
            parts.append(jnp.where(own_entry & (term < ranks), part, 0.0).astype(jnp.bfloat16))
        kept.append(jnp.concatenate(parts, axis=0))
    for (n, g, here), coefficients in zip(batches, kept):
        value = jnp.dot(
            coefficients, weights(far_left, g, here), preferred_element_type=jnp.float32
        )
        for m in range(2):
            part = value[m * sides * half : (m + 1) * sides * half, m * LANES : (m + 1) * LANES]
            for s in range(sides):
                far_out[n, here[m], s * LANES : (s + 1) * LANES] = part[s * half : (s + 1) * half]
    return [split_dot(far_place[g], far_out[n], terms) for n, g in enumerate(chosen)]


def iota(shape, dimension):
    return lax.broadcasted_iota(jnp.int32, shape, dimension)


def to_code(value, scale, top):
    return jnp.floor(jnp.clip(value * (top / scale), -top, top) + 0.5)


def narrow(code):
    return code.astype(jnp.int32).astype(jnp.int16)


def decode(code):
    return code.astype(jnp.int32).astype(jnp.float32)


def largest(value):
    top = jnp.max(jnp.abs(value), axis=0, keepdims=True)
    return jnp.maximum(jnp.max(top, axis=1, keepdims=True), 1e-30)


def total_of(value):
    return jnp.sum(jnp.sum(value, axis=0, keepdims=True), axis=1, keepdims=True)


def arnoldi_kernel(
    rows,
    columns,
    side_ref,
    cluster_ref,
    near_columns_ref,
    near_rows_ref,
    far_columns_ref,
    far_rows_ref,
    far_rank_ref,
    near_hbm,
    far_left_hbm,
    far_right_hbm,
    basis_ref,
    basis_rest_ref,
    next_ref,
    next_rest_ref,
    entries_ref,
    tables,
    near_pick,
    near_place,
    near_picked,
    far_pick,
    far_place,
    far_ranks,
    far_picked,
    sent,
    landed,
    sent_basis,
    landed_basis,
    sent_image,
    landed_image,
    first_ref,
    near_ref,
    far_left,
    far_right,
    own,
    basis,
    image,
    everything,
    extended,
    left,
    right,
    near_out,
    far_out,
    to_partner,
    from_partner,
    to_chips,
    wide_to,
    wide_from,
    code_to,
    code_from,
    scale_to,
    scale_from,
    mine,
    parts,
    load_sem,
    halo_send,
    halo_recv,
    spread_send,
    spread_recv,
    pair_send,
    pair_recv,
    chip_send,
    chip_recv,
    scale_send,
    scale_recv,
    all_send,
    all_recv,
):
    row, column = lax.axis_index("row"), lax.axis_index("col")
    count = rows * columns
    me = row * columns + column
    blocks, width = first_ref.shape
    sides = width // LANES
    halo = left.shape[1]
    groups = far_left.shape[0]
    near_groups = near_ref.shape[0]
    pairs = columns // 2
    chip, core = lax.div(column, 2), lax.rem(column, 2)
    partner = 2 * chip + 1 - core
    panels = count * blocks * LANES
    lanes = [slice(s * LANES, (s + 1) * LANES) for s in range(sides)]
    capacity = (sent.shape[1] - TILE) // sides
    slots = count * capacity
    lane_row = iota((1, LANES), 1)
    some = sides // HALVES
    code_to, code_from = (wide_to, code_to), (wide_from, code_from)
    entered = greet(me, rows, columns)

    def load(kind, g):
        source, target = (
            (near_hbm, near_ref),
            (far_left_hbm, far_left),
            (far_right_hbm, far_right),
        )[kind]
        return pltpu.make_async_copy(source.at[g], target.at[g], load_sem.at[kind, g])

    for kind, many in enumerate((near_groups, groups, groups)):

        @pl.loop(0, many)
        def _(g, kind=kind):
            load(kind, g).start()

    def to_all(n, source, destination, part):
        def copy(peer, there, here):
            return pltpu.make_async_remote_copy(
                src_ref=source.at[there, part],
                dst_ref=destination.at[here, part],
                send_sem=all_send.at[n],
                recv_sem=all_recv.at[n],
                device_id=coordinates(peer, columns),
                device_id_type=MESH,
            )

        def start():
            @pl.loop(1, count)
            def _(k):
                peer = lax.rem(me + k, count)
                copy(peer, peer, me).start()

            destination[me] = source[me]

        every = copy(lax.rem(me + 1, count), pl.ds(0, count - 1), pl.ds(0, count - 1))
        return start, every.wait_recv, every.wait_send

    def share(n, values):
        row_of = jnp.zeros((1, LANES), jnp.float32)
        for place, value in enumerate(values):
            row_of = row_of + jnp.where(lane_row == place, value, 0.0)
        mine[n] = jnp.broadcast_to(row_of, (TILE, LANES))

        def copy(peer, here):
            return pltpu.make_async_remote_copy(
                src_ref=(
                    parts.at[n, pl.ds(0, count - 1), pl.ds(0, 1)]
                    if here is None
                    else mine.at[n, pl.ds(0, 1)]
                ),
                dst_ref=parts.at[n, pl.ds(0, count - 1) if here is None else here, pl.ds(0, 1)],
                send_sem=all_send.at[3 + n],
                recv_sem=all_recv.at[3 + n],
                device_id=coordinates(peer, columns),
                device_id_type=MESH,
            )

        @pl.loop(1, count)
        def _(k):
            copy(lax.rem(me + k, count), me).start()

        parts[n, me] = mine[n]
        every = copy(lax.rem(me + 1, count), None)

        def wait():
            every.wait_recv()
            every.wait_send()
            return parts[n, :, 0, :]

        return wait

    def single(total, place):
        return jnp.sum(jnp.where(lane_row == place, total, 0.0), axis=1, keepdims=True)

    cluster = cluster_ref[...]
    target = lax.div(cluster, blocks)
    turned = jnp.broadcast_to(cluster.astype(jnp.float32), (blocks, blocks)).T.astype(jnp.int32)
    turned_target = lax.div(turned, blocks)
    place = turned - turned_target * blocks
    square = (blocks, blocks)
    same = turned_target == target
    ranks = jnp.where(same & (iota(square, 1) < iota(square, 0)), 1, 0)
    rank_column = jnp.sum(ranks, axis=1, keepdims=True)
    ranks = jnp.where(same & (iota(square, 0) < iota(square, 1)), 1, 0)
    rank_row = jnp.sum(ranks, axis=0, keepdims=True)
    slot_shape = (slots, blocks)
    to_slot = one_hot(iota(slot_shape, 0) == target * capacity + rank_row)
    to_device = one_hot(lax.div(iota(slot_shape, 0), capacity) == target)
    marks = jnp.where(iota(square, 1) == rank_column, place + 1, 0)
    extra = jnp.dot(
        to_device,
        marks.astype(jnp.float32).astype(jnp.bfloat16),
        preferred_element_type=jnp.float32,
    )
    stride = [pl.ds(s, blocks, stride=sides) for s in range(sides)]
    for s in range(sides):
        value = side_ref[stride[s], :]
        extra = extra + jnp.where(lane_row == capacity + s, total_of(value * value), 0.0)
        picked = split_dot(to_slot, value)
        sent[:, s * capacity : (s + 1) * capacity, :] = picked.reshape(count, capacity, LANES)
    top = sides * capacity
    if capacity == TILE:
        sent[:, top:, :] = extra.reshape(count, TILE, LANES)
    else:
        sent[:, top:, :] = extra.reshape(count, capacity, LANES)[:, :TILE]
    entered()
    out_start, out_recv, out_send = to_all(0, sent, landed, pl.ds(0, top + 1))
    out_start()

    near_count, far_count = near_ref.shape[1], far_left.shape[1]

    def turn(g, *sources):
        tables[g] = jnp.zeros(tables.shape[1:], jnp.float32)
        for spot, source in enumerate(sources):
            tables[g, spot : spot + 1, : source.shape[1]] = source.astype(jnp.float32)
        return tables[g].T

    def matches(column, many):
        return one_hot(column == iota((column.shape[0], many), 1).astype(jnp.float32))

    def places(row_of):
        return one_hot(iota((blocks, row_of.shape[1]), 0) == row_of)

    for g in range(near_groups):
        column_of = turn(g, near_columns_ref[g : g + 1])
        near_pick[g] = matches(column_of[:near_count, 0:1], extended.shape[0])
        near_place[g] = places(near_rows_ref[g : g + 1])
    for g in range(groups):
        column_of = turn(near_groups + g, far_columns_ref[g : g + 1], far_rank_ref[g : g + 1])
        far_pick[g] = matches(column_of[:far_count, 0:1], rows * blocks)
        far_ranks[g] = jnp.broadcast_to(column_of[:far_count, 1:2], far_ranks.shape[1:])
        far_place[g] = places(far_rows_ref[g : g + 1] - g * blocks)

    out_recv()
    table = landed[:, top, :]
    total = jnp.sum(table, axis=0, keepdims=True)
    norms = [
        jnp.sqrt(single(total, capacity + s) / panels + epsilon) for s in range(sides)
    ]
    spread_marks = jnp.dot(
        one_hot(lax.div(iota((slots, count), 0), capacity) == iota((slots, count), 1)),
        jnp.where(iota((count, LANES), 1) < capacity, table, 0.0).astype(jnp.bfloat16),
        preferred_element_type=jnp.float32,
    )
    wide = (slots, LANES)
    held = jnp.sum(
        jnp.where(lax.rem(iota(wide, 0), capacity) == iota(wide, 1), spread_marks, 0.0),
        axis=1,
        keepdims=True,
    ).astype(jnp.int32) - 1
    to_mesh_wide = jnp.where(held == iota((slots, blocks), 1), 1.0, 0.0)
    to_mesh = to_mesh_wide.astype(jnp.bfloat16)
    to_cluster = to_mesh_wide.T.astype(jnp.bfloat16)
    for s in range(sides):
        arrived = landed[:, s * capacity : (s + 1) * capacity, :].reshape(slots, LANES)
        value = split_dot(to_cluster, arrived) / norms[s]
        first_ref[:, lanes[s]] = value
        own[s // some, :, lanes[s % some]] = value.astype(jnp.bfloat16)
    out_send()

    part_width = width // HALVES
    parts_of = [slice(h * part_width, (h + 1) * part_width) for h in range(HALVES)]

    def operate(a, prepare, between):
        after = coordinates(lax.rem(me + 1, count), columns)
        before = coordinates(lax.rem(me + count - 1, count), columns)
        halos = [
            remote(
                own.at[:, pl.ds(blocks - halo, halo)],
                left,
                halo_send.at[a],
                halo_recv.at[a],
                0,
                after,
            ),
            remote(own.at[:, pl.ds(0, halo)], right, halo_send.at[a], halo_recv.at[a], 1, before),
        ]
        for copy in halos:
            copy.start()
        for h in range(HALVES):
            everything[h, row] = own[h]

        def inside(index):
            return (index >= 0) & (index < rows)

        def hop(h, way, distance, source):
            sign = 1 - 2 * way
            reach = 2 if distance == 2 else 1
            return remote(
                everything.at[h, source],
                everything.at[h, source],
                spread_send.at[a, h, way],
                spread_recv.at[a, h, way],
                distance - 1,
                (lax.rem(row + sign * reach + 2 * rows, rows), column),
            )

        def arrive(h, distance):
            for way in range(2):
                source = row - (1 - 2 * way) * distance

                @pl.when(inside(source))
                def _(way=way, source=source):
                    hop(h, way, distance, source).wait_recv()

        def each_hop(h, distance, act):
            for way in range(2):
                sign = 1 - 2 * way
                held_at = 0 if distance < 3 else distance - 1
                source = row - sign * held_at
                there = row + sign * (2 if distance == 2 else 1)

                @pl.when(inside(source) & inside(there))
                def _(way=way, source=source):
                    act(hop(h, way, distance, source))

        def begin(copy):
            copy.start()

        for h in range(HALVES):
            for distance in reversed(range(1, min(rows, 3))):
                each_hop(h, distance, begin)
        image[...] = 0.5 * basis_or_first[a][...].astype(jnp.bfloat16).astype(jnp.float32)
        for h in range(HALVES):
            extended[halo : halo + blocks, parts_of[h]] = own[h]
        for distance in range(3, rows):
            for h in range(HALVES):
                arrive(h, distance - 1)
                each_hop(h, distance, begin)
        for copy in halos:
            copy.wait()
        for h in range(HALVES):
            extended[0:halo, parts_of[h]] = left[h]
            extended[halo + blocks :, parts_of[h]] = right[h]
        for g in range(near_groups):
            near_picked[g] = jnp.dot(
                near_pick[g], extended[...], preferred_element_type=jnp.float32
            )

        def near(g):
            if a == 0:
                load(0, g).wait()
            near_group(sides, g, near_picked, near_place, near_ref, near_out, image, 3 - a)

        prepare()
        if a == 0:
            for kind in (1, 2):

                @pl.loop(0, groups)
                def _(g, kind=kind):
                    load(kind, g).wait()

        far = functools.partial(
            far_group,
            some,
            3 - a,
            far_place=far_place,
            far_ranks=far_ranks,
            far_left=far_left,
            far_right=far_right,
            far_out=far_out,
        )

        def pair_copy(h, k, q):
            return remote(
                to_partner.at[h, q],
                from_partner.at[h, q],
                pair_send.at[a, h],
                pair_recv.at[a, h],
                k,
                (row, partner),
            )

        def chip_copies(h, k, q, here):
            device = (row, 2 * q + core)
            return [
                remote(
                    code_to[a].at[h, q],
                    code_from[a].at[h, here],
                    chip_send.at[a, h],
                    chip_recv.at[a, h],
                    k,
                    device,
                ),
                remote(
                    scale_to.at[a, h, q],
                    scale_from.at[a, h, here],
                    scale_send.at[a, h],
                    scale_recv.at[a, h],
                    k,
                    device,
                ),
            ]

        top_code = WIDE if a == 0 else TOP

        def pack(h, q):
            lows = []
            for s in range(some):
                value = to_chips[h, q, :, lanes[s]]
                scale = jnp.maximum(jnp.max(jnp.abs(value), axis=0, keepdims=True), 1e-30)
                scale_to[a, h, q, s * TILE : (s + 1) * TILE] = jnp.broadcast_to(
                    scale, (TILE, LANES)
                )
                code = to_code(value, scale, top_code)
                if a == 0:
                    high = jnp.floor(code * (1.0 / BYTE))
                    lows.append(code - high * BYTE)
                    code = high
                code_to[a][h, q, :, lanes[s]] = narrow(code)
            for n in range(len(lows) // 2):
                code = lows[2 * n] * BYTE + (lows[2 * n + 1] - BYTE * BYTE / 2)
                code_to[a][h, q, :, lanes[some + n]] = narrow(code)

        def unpack(h, q):
            codes = [decode(code_from[a][h, q, :, lanes[s]]) for s in range(some)]
            if a == 0:
                for n in range(some // 2):
                    both = decode(code_from[a][h, q, :, lanes[some + n]])
                    both = both + BYTE * BYTE / 2
                    high = jnp.floor(both * (1.0 / BYTE))
                    codes[2 * n] = codes[2 * n] * BYTE + high
                    codes[2 * n + 1] = codes[2 * n + 1] * BYTE + (both - high * BYTE)
            for s in range(some):
                scale = scale_from[a, h, q, s * TILE : s * TILE + 1] * (1.0 / top_code)
                image[:, lanes[h * some + s]] += codes[s] * scale

        for h in range(HALVES):
            for distance in sorted({1, rows - 1}):
                arrive(h, distance)
            for g in range(groups):
                far_picked[h, g] = jnp.dot(
                    far_pick[g],
                    everything[h].reshape(rows * blocks, part_width),
                    preferred_element_type=jnp.float32,
                ).astype(jnp.bfloat16)

            for t in range(1, pairs + 1, 2):
                chosen = [lax.rem(chip + n, pairs) for n in (t, t + 1)]
                found = far(
                    [2 * q + 1 - core for q in chosen] + [2 * q + core for q in chosen],
                    far_picked=far_picked.at[h],
                )
                for n, q in enumerate(chosen):
                    to_partner[h, q] = found[n]
                    pair_copy(h, t + n - 1, q).start()
                    to_chips[h, q] = found[2 + n]

                @pl.loop(t - 2 if t > 1 else 1, t if t < pairs - 1 else pairs + 1)
                def _(i, h=h):
                    q = lax.rem(chip + i, pairs)
                    pair_copy(h, i - 1, q).wait_recv()
                    to_chips[h, q] = to_chips[h, q] + from_partner[h, q]

                    @pl.when(i < pairs)
                    def _():
                        pack(h, q)
                        for copy in chip_copies(h, i - 1, q, chip):
                            copy.start()

            if h == HALVES - 1:
                between()

                @pl.loop(0, near_groups)
                def _(g):
                    near(g)

        for h in range(HALVES):
            image[:, parts_of[h]] += to_chips[h, chip]
            for i in range(1, pairs):
                source = lax.rem(chip + pairs - i, pairs)
                for copy in chip_copies(h, i - 1, source, source):
                    copy.wait_recv()
                unpack(h, source)
        for h in range(HALVES):
            for distance in range(1, rows):
                each_hop(h, distance, lambda copy: copy.wait_send())
            for i in range(1, pairs + 1):
                q = lax.rem(chip + i, pairs)
                pair_copy(h, i - 1, q).wait_send()
                if i < pairs:
                    for copy in chip_copies(h, i - 1, q, chip):
                        copy.wait_send()

    basis_or_first = (first_ref, basis)

    def slot_codes(value, scales, buffer):
        for s in range(0, sides, 2):
            codes = []
            for side in (s, s + 1):
                code = to_code(value[:, lanes[side]], scales[side], TOP)
                codes.append(split_dot(to_mesh, code, 2).reshape(count, capacity, LANES))
            both = jnp.concatenate(codes, axis=1)
            buffer[:, s * capacity : (s + 2) * capacity, :] = narrow(both)

    to_own = one_hot(
        turned_target[:, 0:1] * capacity + rank_column == iota((blocks, slots), 1)
    )
    to_source = one_hot(turned_target[:, 0:1] == iota((blocks, count), 1))

    def home(buffer, scales):
        values = []
        own_scales = split_dot(to_source, scales)
        for s in range(0, sides, 2):
            both = decode(buffer[:, s * capacity : (s + 2) * capacity, :])
            for side in (s, s + 1):
                code = both[:, (side - s) * capacity : (side - s + 1) * capacity]
                code = code.reshape(slots, LANES)
                high = code.astype(jnp.bfloat16)
                scale = own_scales[:, side : side + 1] * (1.0 / TOP)
                values.append(
                    (
                        split_dot(to_own, high, 1) * scale,
                        split_dot(to_own, code - high.astype(jnp.float32), 1) * scale,
                    )
                )
        return values

    operate(0, lambda: None, lambda: None)
    found = [[] for _ in range(7)]
    for s in range(sides):
        one, two = first_ref[:, lanes[s]], image[:, lanes[s]]
        along, size = total_of(one * two), total_of(one * one)
        guess = jnp.where(size > 1e-30, along / jnp.maximum(size, 1e-30), 0.0)
        rest = two - guess * one
        for place, value in enumerate(
            (
                along,
                guess,
                total_of(one * rest),
                total_of(rest * rest),
                size,
                largest(two),
                largest(one),
            )
        ):
            found[place].append(value)
    table = share(0, [value for values in found for value in values])()
    total = jnp.sum(table, axis=0, keepdims=True)
    projects, seconds, basis_scale = [], [], jnp.zeros((count, LANES), jnp.float32)
    for s in range(sides):
        guess, cross, rest, size, top_image, top_first = [
            table[:, n * sides + s : n * sides + s + 1] for n in range(1, 7)
        ]
        project = single(total, s) / panels
        off = guess - project
        norm = jnp.sqrt(
            jnp.sum(rest + off * (2.0 * cross + off * size), axis=0, keepdims=True) / panels
            + epsilon
        )
        value = (image[:, lanes[s]] - project * first_ref[:, lanes[s]]) / norm
        basis[:, lanes[s]] = value
        own[s // some, :, lanes[s % some]] = value.astype(jnp.bfloat16)
        bound = (top_image + jnp.abs(project) * top_first) / norm
        basis_scale = basis_scale + jnp.where(iota((count, LANES), 1) == s, bound, 0.0)
        projects.append(project)
        seconds.append(norm)
    mine_scale = jnp.sum(
        jnp.where(iota((count, LANES), 0) == me, basis_scale, 0.0), axis=0, keepdims=True
    )
    every = pl.ds(0, sides * capacity)
    basis_start, basis_recv, basis_send = to_all(1, sent_basis, landed_basis, every)
    image_start, image_recv, image_send = to_all(2, sent_image, landed_image, every)

    def code_basis():
        slot_codes(basis[...], [single(mine_scale, s) for s in range(sides)], sent_basis)

    operate(1, code_basis, basis_start)
    scales = [largest(image[:, lanes[s]]) for s in range(sides)]
    slot_codes(image[...], scales, sent_image)
    image_start()
    values = []
    for source in (first_ref, basis):
        for s in range(sides):
            values.append(total_of(source[:, lanes[s]] * image[:, lanes[s]]))
    wait = share(1, values + scales)
    basis_recv()
    returned = home(landed_basis, basis_scale)
    for s in range(sides):
        basis_ref[stride[s], :], basis_rest_ref[stride[s], :] = returned[s]
    table = wait()
    total = jnp.sum(table, axis=0, keepdims=True) / panels
    ends = [[single(total, n * sides + s) for s in range(sides)] for n in range(2)]
    for s in range(sides):
        line = jnp.zeros((1, LANES), jnp.float32)
        for place, found in enumerate((norms, projects, seconds, ends[0], ends[1])):
            line = line + jnp.where(lane_row == place, found[s], 0.0)
        entries_ref[s : s + 1] = line[:, : entries_ref.shape[1]]
    kept = iota((count, LANES), 1)
    image_scale = jnp.zeros((count, LANES), jnp.float32)
    for s in range(sides):
        image_scale = image_scale + jnp.where(
            kept == s, table[:, 2 * sides + s : 2 * sides + s + 1], 0.0
        )
    image_recv()
    landed_values = home(landed_image, image_scale)
    for s in range(sides):
        high, rest = landed_values[s]
        next_ref[stride[s], :] = high + rest - ends[0][s] * (side_ref[stride[s], :] / norms[s])
        next_rest_ref[stride[s], :] = ends[1][s] * (returned[s][0] + returned[s][1])
    basis_send()
    image_send()


def body(
    right_side,
    cluster_of,
    near_rows,
    near_columns,
    near_blocks,
    far_rows,
    far_columns,
    far_rank,
    far_left,
    far_right,
):
    rows = lax.axis_size("row")
    columns = lax.axis_size("col")
    count = rows * columns
    blocks, sides, lanes = right_side.shape
    width = sides * lanes
    capacity = max(TILE, 2 * blocks // count)
    near_groups = near_rows.shape[0] // lanes
    near_blocks = near_blocks.reshape(near_groups, -1, *near_blocks.shape[1:])
    far_left = far_left.reshape(columns, -1, *far_left.shape[1:])
    far_right = far_right.reshape(columns, -1, *far_right.shape[1:])
    near_count, far_count = near_blocks.shape[1], far_left.shape[1]
    halo = blocks // 4
    pairs = columns // 2
    part = width // HALVES
    dma = pltpu.SemaphoreType.DMA
    real, half, code = jnp.float32, jnp.bfloat16, jnp.int16
    out_slots = (count, sides * capacity + TILE, lanes)
    code_slots = (count, sides * capacity, lanes)
    hbm = pl.BlockSpec(memory_space=pl.ANY)
    basis, basis_rest, following, following_rest, entries = pl.pallas_call(
        functools.partial(arnoldi_kernel, rows, columns),
        out_shape=[
            *[jax.ShapeDtypeStruct((blocks * sides, lanes), real)] * 4,
            jax.ShapeDtypeStruct((sides, 5), real),
        ],
        in_specs=[VMEM] * 7 + [hbm] * 3,
        out_specs=[VMEM] * 5,
        scratch_shapes=[
            pltpu.VMEM((near_groups + columns, TILE, lanes), real),
            pltpu.VMEM((near_groups, near_count, blocks + 2 * halo), half),
            pltpu.VMEM((near_groups, blocks, near_count), half),
            pltpu.VMEM((near_groups, near_count, width), real),
            pltpu.VMEM((columns, far_count, rows * blocks), half),
            pltpu.VMEM((columns, blocks, far_count), half),
            pltpu.VMEM((columns, far_count, lanes), real),
            pltpu.VMEM((HALVES, columns, far_count, part), half),
            pltpu.VMEM(out_slots, real),
            pltpu.VMEM(out_slots, real),
            pltpu.VMEM(code_slots, code),
            pltpu.VMEM(code_slots, code),
            pltpu.VMEM(code_slots, code),
            pltpu.VMEM(code_slots, code),
            pltpu.VMEM((blocks, width), real),
            pltpu.VMEM(near_blocks.shape, half),
            pltpu.VMEM(far_left.shape, half),
            pltpu.VMEM(far_right.shape, half),
            pltpu.VMEM((HALVES, blocks, part), half),
            pltpu.VMEM((blocks, width), real),
            pltpu.VMEM((blocks, width), real),
            pltpu.VMEM((HALVES, rows, blocks, part), half),
            pltpu.VMEM((blocks + 2 * halo, width), half),
            pltpu.VMEM((HALVES, halo, part), half),
            pltpu.VMEM((HALVES, halo, part), half),
            pltpu.VMEM((near_count, width), real),
            pltpu.VMEM((4, far_count, part), real),
            pltpu.VMEM((HALVES, pairs, blocks, part), real),
            pltpu.VMEM((HALVES, pairs, blocks, part), real),
            pltpu.VMEM((HALVES, pairs, blocks, part), real),
            pltpu.VMEM((HALVES, pairs, blocks, 3 * part // 2), code),
            pltpu.VMEM((HALVES, pairs, blocks, 3 * part // 2), code),
            pltpu.VMEM((HALVES, pairs, blocks, part), code),
            pltpu.VMEM((HALVES, pairs, blocks, part), code),
            pltpu.VMEM((2, HALVES, pairs, sides // HALVES * TILE, lanes), real),
            pltpu.VMEM((2, HALVES, pairs, sides // HALVES * TILE, lanes), real),
            pltpu.VMEM((2, TILE, lanes), real),
            pltpu.VMEM((2, count, TILE, lanes), real),
            dma((3, max(columns, near_groups))),
            dma((2, 2)),
            dma((2, 2)),
            dma((2, HALVES, 2, rows - 1)),
            dma((2, HALVES, 2, rows - 1)),
            dma((2, HALVES, pairs)),
            dma((2, HALVES, pairs)),
            dma((2, HALVES, pairs)),
            dma((2, HALVES, pairs)),
            dma((2, HALVES, pairs)),
            dma((2, HALVES, pairs)),
            dma((5,)),
            dma((5,)),
        ],
        compiler_params=pltpu.CompilerParams(
            collective_id=0, has_side_effects=True, vmem_limit_bytes=LIMIT
        ),
    )(
        right_side.reshape(blocks * sides, lanes),
        cluster_of.reshape(1, blocks),
        near_columns.reshape(near_groups, -1),
        near_rows.reshape(near_groups, -1),
        far_columns.reshape(columns, -1),
        far_rows.reshape(columns, -1),
        far_rank.reshape(columns, -1),
        near_blocks,
        far_left,
        far_right,
    )
    shape = (blocks, sides, lanes)
    return (
        (basis + basis_rest).reshape(shape),
        (following - following_rest).reshape(shape),
        entries.T,
    )


def solution(mesh):
    vector = P(("row", "col"), None, None)
    table = P(("row", "col"))
    placed = (vector, table, table, table, vector, table, table, table, vector, vector)
    return jax.shard_map(
        body,
        mesh=mesh,
        in_specs=placed,
        out_specs=(vector, vector, P()),
        check_vma=False,
    )
```

```python
import functools

import jax
import jax.numpy as jnp
from jax import lax
from jax.experimental import pallas as pl
from jax.experimental.pallas import tpu as pltpu
from jax.sharding import PartitionSpec as P

epsilon = 1e-06
MESH = pl.DeviceIdType.MESH
VMEM = pl.BlockSpec(memory_space=pltpu.VMEM)
LANES = 128
LIMIT = 56 * 2**20
TILE = 8
TOP = 32767.0
WIDE = 8388607.0
BYTE = 256.0
HALVES = 2


def coordinates(index, column_count):
    return (lax.div(index, column_count), lax.rem(index, column_count))


def greet(me, rows, columns):
    count = rows * columns
    barrier = pltpu.get_barrier_semaphore()

    @pl.loop(1, count)
    def _(k):
        pl.semaphore_signal(
            barrier,
            inc=1,
            device_id=coordinates(lax.rem(me + k, count), columns),
            device_id_type=MESH,
        )

    return functools.partial(pl.semaphore_wait, barrier, count - 1)


def split_dot(picker, value, terms=3):
    parts = []
    for _ in range(terms):
        parts.append(value.astype(jnp.bfloat16))
        value = value - parts[-1].astype(jnp.float32)
    dot = functools.partial(jnp.dot, preferred_element_type=jnp.float32)
    if picker.shape[1] % LANES == 0:
        return dot(jnp.concatenate([picker] * terms, axis=1), jnp.concatenate(parts, axis=0))
    return sum(dot(picker, part) for part in parts)


def one_hot(condition):
    return jnp.where(condition, 1.0, 0.0).astype(jnp.bfloat16)


def remote(source, destination, sends, recvs, k, device):
    return pltpu.make_async_remote_copy(
        src_ref=source,
        dst_ref=destination,
        send_sem=sends.at[k],
        recv_sem=recvs.at[k],
        device_id=device,
        device_id_type=MESH,
    )


def corners(one, two):
    empty = jnp.zeros_like(one)
    return jnp.concatenate(
        [jnp.concatenate([one, empty], axis=1), jnp.concatenate([empty, two], axis=1)], axis=0
    )


def near_group(sides, g, near_picked, near_place, near_ref, near_out, image, terms):
    near_count = near_ref.shape[1]
    half = 8
    both = 2 * half
    shape = (sides * half, LANES)
    row_id = lax.rem(lax.broadcasted_iota(jnp.int32, shape, 0), half)
    for j in range(near_count // both):
        here = [slice(j * both + n * half, j * both + (n + 1) * half) for n in range(2)]
        rows = [
            jnp.concatenate(
                [near_picked[g, here[n], s * LANES : (s + 1) * LANES] for s in range(sides)],
                axis=0,
            ).astype(jnp.bfloat16)
            for n in range(2)
        ]
        weights = jnp.concatenate(
            [near_ref[g, here[n]].reshape(half * LANES, LANES) for n in range(2)], axis=1
        )
        product = lax.dot_general(
            corners(*rows), weights, (((1,), (1,)), ((), ())), preferred_element_type=jnp.float32
        )
        for n in range(2):
            part = product[n * sides * half : (n + 1) * sides * half]
            value = part[:, :LANES]
            for e in range(1, half):
                value = jnp.where(row_id == e, part[:, e * LANES : (e + 1) * LANES], value)
            for s in range(sides):
                near_out[here[n], s * LANES : (s + 1) * LANES] = value[s * half : (s + 1) * half]
    image[...] += split_dot(near_place[g], near_out[...], terms)


def far_group(
    sides, terms, chosen, far_picked, far_place, far_ranks, far_left, far_right, far_out
):
    far_count, rank = far_left.shape[1:3]
    half = 16
    both = 2 * half
    shape = (sides * half, half * rank)
    entry = lax.rem(lax.broadcasted_iota(jnp.int32, shape, 0), half)
    lane = lax.broadcasted_iota(jnp.int32, shape, 1)
    term = lax.rem(lane, rank).astype(jnp.float32)
    own_entry = lax.div(lane, rank) == entry
    kept = []
    batches = [
        (n, g, [slice(j * both + m * half, j * both + (m + 1) * half) for m in range(2)])
        for n, g in enumerate(chosen)
        for j in range(far_count // both)
    ]

    def weights(factor, g, here):
        return jnp.concatenate(
            [factor[g, part].reshape(half * rank, LANES) for part in here], axis=1
        )

    for _, g, here in batches:
        rows = [
            jnp.concatenate(
                [far_picked[g, part, s * LANES : (s + 1) * LANES] for s in range(sides)], axis=0
            )
            for part in here
        ]
        product = lax.dot_general(
            corners(*rows),
            weights(far_right, g, here),
            (((1,), (1,)), ((), ())),
            preferred_element_type=jnp.float32,
        )
        parts = []
        for m in range(2):
            ranks = jnp.concatenate([far_ranks[g, here[m], 0:1]] * sides, axis=0)
            part = product[m * sides * half : (m + 1) * sides * half]
            parts.append(jnp.where(own_entry & (term < ranks), part, 0.0).astype(jnp.bfloat16))
        kept.append(jnp.concatenate(parts, axis=0))
    for (n, g, here), coefficients in zip(batches, kept):
        value = jnp.dot(
            coefficients, weights(far_left, g, here), preferred_element_type=jnp.float32
        )
        for m in range(2):
            part = value[m * sides * half : (m + 1) * sides * half, m * LANES : (m + 1) * LANES]
            for s in range(sides):
                far_out[n, here[m], s * LANES : (s + 1) * LANES] = part[s * half : (s + 1) * half]
    return [split_dot(far_place[g], far_out[n], terms) for n, g in enumerate(chosen)]


def iota(shape, dimension):
    return lax.broadcasted_iota(jnp.int32, shape, dimension)


def to_code(value, scale, top):
    return jnp.floor(jnp.clip(value * (top / scale), -top, top) + 0.5)


def narrow(code):
    return code.astype(jnp.int32).astype(jnp.int16)


def decode(code):
    return code.astype(jnp.int32).astype(jnp.float32)


def largest(value):
    top = jnp.max(jnp.abs(value), axis=0, keepdims=True)
    return jnp.maximum(jnp.max(top, axis=1, keepdims=True), 1e-30)


def total_of(value):
    return jnp.sum(jnp.sum(value, axis=0, keepdims=True), axis=1, keepdims=True)


def arnoldi_kernel(
    rows,
    columns,
    side_ref,
    cluster_ref,
    near_columns_ref,
    near_rows_ref,
    far_columns_ref,
    far_rows_ref,
    far_rank_ref,
    near_hbm,
    far_left_hbm,
    far_right_hbm,
    basis_ref,
    basis_rest_ref,
    next_ref,
    next_rest_ref,
    entries_ref,
    tables,
    near_pick,
    near_place,
    near_picked,
    far_pick,
    far_place,
    far_ranks,
    far_picked,
    sent,
    landed,
    sent_basis,
    landed_basis,
    sent_image,
    landed_image,
    first_ref,
    near_ref,
    far_left,
    far_right,
    own,
    basis,
    image,
    everything,
    extended,
    left,
    right,
    near_out,
    far_out,
    to_partner,
    from_partner,
    to_chips,
    wide_to,
    wide_from,
    code_to,
    code_from,
    scale_to,
    scale_from,
    mine,
    parts,
    load_sem,
    halo_send,
    halo_recv,
    spread_send,
    spread_recv,
    pair_send,
    pair_recv,
    chip_send,
    chip_recv,
    scale_send,
    scale_recv,
    all_send,
    all_recv,
):
    row, column = lax.axis_index("row"), lax.axis_index("col")
    count = rows * columns
    me = row * columns + column
    blocks, width = first_ref.shape
    sides = width // LANES
    halo = left.shape[1]
    groups = far_left.shape[0]
    near_groups = near_ref.shape[0]
    pairs = columns // 2
    chip, core = lax.div(column, 2), lax.rem(column, 2)
    partner = 2 * chip + 1 - core
    panels = count * blocks * LANES
    lanes = [slice(s * LANES, (s + 1) * LANES) for s in range(sides)]
    capacity = (sent.shape[1] - TILE) // sides
    slots = count * capacity
    lane_row = iota((1, LANES), 1)
    some = sides // HALVES
    code_to, code_from = (wide_to, code_to), (wide_from, code_from)
    entered = greet(me, rows, columns)

    def load(kind, g):
        source, target = (
            (near_hbm, near_ref),
            (far_left_hbm, far_left),
            (far_right_hbm, far_right),
        )[kind]
        return pltpu.make_async_copy(source.at[g], target.at[g], load_sem.at[kind, g])

    for kind, many in enumerate((near_groups, groups, groups)):

        @pl.loop(0, many)
        def _(g, kind=kind):
            load(kind, g).start()

    def to_all(n, source, destination, part):
        def copy(peer, there, here):
            return pltpu.make_async_remote_copy(
                src_ref=source.at[there, part],
                dst_ref=destination.at[here, part],
                send_sem=all_send.at[n],
                recv_sem=all_recv.at[n],
                device_id=coordinates(peer, columns),
                device_id_type=MESH,
            )

        def start():
            @pl.loop(1, count)
            def _(k):
                peer = lax.rem(me + k, count)
                copy(peer, peer, me).start()

            destination[me] = source[me]

        every = copy(lax.rem(me + 1, count), pl.ds(0, count - 1), pl.ds(0, count - 1))
        return start, every.wait_recv, every.wait_send

    def share(n, values):
        row_of = jnp.zeros((1, LANES), jnp.float32)
        for place, value in enumerate(values):
            row_of = row_of + jnp.where(lane_row == place, value, 0.0)
        mine[n] = jnp.broadcast_to(row_of, (TILE, LANES))

        def copy(peer, here):
            return pltpu.make_async_remote_copy(
                src_ref=(
                    parts.at[n, pl.ds(0, count - 1), pl.ds(0, 1)]
                    if here is None
                    else mine.at[n, pl.ds(0, 1)]
                ),
                dst_ref=parts.at[n, pl.ds(0, count - 1) if here is None else here, pl.ds(0, 1)],
                send_sem=all_send.at[3 + n],
                recv_sem=all_recv.at[3 + n],
                device_id=coordinates(peer, columns),
                device_id_type=MESH,
            )

        @pl.loop(1, count)
        def _(k):
            copy(lax.rem(me + k, count), me).start()

        parts[n, me] = mine[n]
        every = copy(lax.rem(me + 1, count), None)

        def wait():
            every.wait_recv()
            every.wait_send()
            return parts[n, :, 0, :]

        return wait

    def single(total, place):
        return jnp.sum(jnp.where(lane_row == place, total, 0.0), axis=1, keepdims=True)

    cluster = cluster_ref[...]
    target = lax.div(cluster, blocks)
    turned = jnp.broadcast_to(cluster.astype(jnp.float32), (blocks, blocks)).T.astype(jnp.int32)
    turned_target = lax.div(turned, blocks)
    place = turned - turned_target * blocks
    square = (blocks, blocks)
    same = turned_target == target
    ranks = jnp.where(same & (iota(square, 1) < iota(square, 0)), 1, 0)
    rank_column = jnp.sum(ranks, axis=1, keepdims=True)
    ranks = jnp.where(same & (iota(square, 0) < iota(square, 1)), 1, 0)
    rank_row = jnp.sum(ranks, axis=0, keepdims=True)
    slot_shape = (slots, blocks)
    to_slot = one_hot(iota(slot_shape, 0) == target * capacity + rank_row)
    to_device = one_hot(lax.div(iota(slot_shape, 0), capacity) == target)
    marks = jnp.where(iota(square, 1) == rank_column, place + 1, 0)
    extra = jnp.dot(
        to_device,
        marks.astype(jnp.float32).astype(jnp.bfloat16),
        preferred_element_type=jnp.float32,
    )
    stride = [pl.ds(s, blocks, stride=sides) for s in range(sides)]
    for s in range(sides):
        value = side_ref[stride[s], :]
        extra = extra + jnp.where(lane_row == capacity + s, total_of(value * value), 0.0)
        picked = split_dot(to_slot, value)
        sent[:, s * capacity : (s + 1) * capacity, :] = picked.reshape(count, capacity, LANES)
    top = sides * capacity
    if capacity == TILE:
        sent[:, top:, :] = extra.reshape(count, TILE, LANES)
    else:
        sent[:, top:, :] = extra.reshape(count, capacity, LANES)[:, :TILE]
    entered()
    out_start, out_recv, out_send = to_all(0, sent, landed, pl.ds(0, top + 1))
    out_start()

    near_count, far_count = near_ref.shape[1], far_left.shape[1]

    def turn(g, *sources):
        tables[g] = jnp.zeros(tables.shape[1:], jnp.float32)
        for spot, source in enumerate(sources):
            tables[g, spot : spot + 1, : source.shape[1]] = source.astype(jnp.float32)
        return tables[g].T

    def matches(column, many):
        return one_hot(column == iota((column.shape[0], many), 1).astype(jnp.float32))

    def places(row_of):
        return one_hot(iota((blocks, row_of.shape[1]), 0) == row_of)

    for g in range(near_groups):
        column_of = turn(g, near_columns_ref[g : g + 1])
        near_pick[g] = matches(column_of[:near_count, 0:1], extended.shape[0])
        near_place[g] = places(near_rows_ref[g : g + 1])
    for g in range(groups):
        column_of = turn(near_groups + g, far_columns_ref[g : g + 1], far_rank_ref[g : g + 1])
        far_pick[g] = matches(column_of[:far_count, 0:1], rows * blocks)
        far_ranks[g] = jnp.broadcast_to(column_of[:far_count, 1:2], far_ranks.shape[1:])
        far_place[g] = places(far_rows_ref[g : g + 1] - g * blocks)

    out_recv()
    table = landed[:, top, :]
    total = jnp.sum(table, axis=0, keepdims=True)
    norms = [
        jnp.sqrt(single(total, capacity + s) / panels + epsilon) for s in range(sides)
    ]
    spread_marks = jnp.dot(
        one_hot(lax.div(iota((slots, count), 0), capacity) == iota((slots, count), 1)),
        jnp.where(iota((count, LANES), 1) < capacity, table, 0.0).astype(jnp.bfloat16),
        preferred_element_type=jnp.float32,
    )
    wide = (slots, LANES)
    held = jnp.sum(
        jnp.where(lax.rem(iota(wide, 0), capacity) == iota(wide, 1), spread_marks, 0.0),
        axis=1,
        keepdims=True,
    ).astype(jnp.int32) - 1
    to_mesh_wide = jnp.where(held == iota((slots, blocks), 1), 1.0, 0.0)
    to_mesh = to_mesh_wide.astype(jnp.bfloat16)
    to_cluster = to_mesh_wide.T.astype(jnp.bfloat16)
    for s in range(sides):
        arrived = landed[:, s * capacity : (s + 1) * capacity, :].reshape(slots, LANES)
        value = split_dot(to_cluster, arrived) / norms[s]
        first_ref[:, lanes[s]] = value
        own[s // some, :, lanes[s % some]] = value.astype(jnp.bfloat16)
    out_send()

    part_width = width // HALVES
    parts_of = [slice(h * part_width, (h + 1) * part_width) for h in range(HALVES)]

    def operate(a, prepare, between):
        after = coordinates(lax.rem(me + 1, count), columns)
        before = coordinates(lax.rem(me + count - 1, count), columns)
        halos = [
            remote(
                own.at[:, pl.ds(blocks - halo, halo)],
                left,
                halo_send.at[a],
                halo_recv.at[a],
                0,
                after,
            ),
            remote(own.at[:, pl.ds(0, halo)], right, halo_send.at[a], halo_recv.at[a], 1, before),
        ]
        for copy in halos:
            copy.start()
        for h in range(HALVES):
            everything[h, row] = own[h]

        def inside(index):
            return (index >= 0) & (index < rows)

        def hop(h, way, distance, source):
            sign = 1 - 2 * way
            reach = 2 if distance == 2 else 1
            return remote(
                everything.at[h, source],
                everything.at[h, source],
                spread_send.at[a, h, way],
                spread_recv.at[a, h, way],
                distance - 1,
                (lax.rem(row + sign * reach + 2 * rows, rows), column),
            )

        def arrive(h, distance):
            for way in range(2):
                source = row - (1 - 2 * way) * distance

                @pl.when(inside(source))
                def _(way=way, source=source):
                    hop(h, way, distance, source).wait_recv()

        def each_hop(h, distance, act):
            for way in range(2):
                sign = 1 - 2 * way
                held_at = 0 if distance < 3 else distance - 1
                source = row - sign * held_at
                there = row + sign * (2 if distance == 2 else 1)

                @pl.when(inside(source) & inside(there))
                def _(way=way, source=source):
                    act(hop(h, way, distance, source))

        def begin(copy):
            copy.start()

        for h in range(HALVES):
            for distance in reversed(range(1, min(rows, 3))):
                each_hop(h, distance, begin)
        image[...] = 0.5 * basis_or_first[a][...].astype(jnp.bfloat16).astype(jnp.float32)
        for h in range(HALVES):
            extended[halo : halo + blocks, parts_of[h]] = own[h]
        for distance in range(3, rows):
            for h in range(HALVES):
                arrive(h, distance - 1)
                each_hop(h, distance, begin)
        for copy in halos:
            copy.wait()
        for h in range(HALVES):
            extended[0:halo, parts_of[h]] = left[h]
            extended[halo + blocks :, parts_of[h]] = right[h]
        for g in range(near_groups):
            near_picked[g] = jnp.dot(
                near_pick[g], extended[...], preferred_element_type=jnp.float32
            )

        def near(g):
            if a == 0:
                load(0, g).wait()
            near_group(sides, g, near_picked, near_place, near_ref, near_out, image, 3 - a)

        prepare()
        if a == 0:
            for kind in (1, 2):

                @pl.loop(0, groups)
                def _(g, kind=kind):
                    load(kind, g).wait()

        far = functools.partial(
            far_group,
            some,
            3 - a,
            far_place=far_place,
            far_ranks=far_ranks,
            far_left=far_left,
            far_right=far_right,
            far_out=far_out,
        )

        def pair_copy(h, k, q):
            return remote(
                to_partner.at[h, q],
                from_partner.at[h, q],
                pair_send.at[a, h],
                pair_recv.at[a, h],
                k,
                (row, partner),
            )

        def chip_copies(h, k, q, here):
            device = (row, 2 * q + core)
            return [
                remote(
                    code_to[a].at[h, q],
                    code_from[a].at[h, here],
                    chip_send.at[a, h],
                    chip_recv.at[a, h],
                    k,
                    device,
                ),
                remote(
                    scale_to.at[a, h, q],
                    scale_from.at[a, h, here],
                    scale_send.at[a, h],
                    scale_recv.at[a, h],
                    k,
                    device,
                ),
            ]

        top_code = WIDE if a == 0 else TOP

        def pack(h, q):
            lows = []
            for s in range(some):
                value = to_chips[h, q, :, lanes[s]]
                scale = jnp.maximum(jnp.max(jnp.abs(value), axis=0, keepdims=True), 1e-30)
                scale_to[a, h, q, s * TILE : (s + 1) * TILE] = jnp.broadcast_to(
                    scale, (TILE, LANES)
                )
                code = to_code(value, scale, top_code)
                if a == 0:
                    high = jnp.floor(code * (1.0 / BYTE))
                    lows.append(code - high * BYTE)
                    code = high
                code_to[a][h, q, :, lanes[s]] = narrow(code)
            for n in range(len(lows) // 2):
                code = lows[2 * n] * BYTE + (lows[2 * n + 1] - BYTE * BYTE / 2)
                code_to[a][h, q, :, lanes[some + n]] = narrow(code)

        def unpack(h, q):
            codes = [decode(code_from[a][h, q, :, lanes[s]]) for s in range(some)]
            if a == 0:
                for n in range(some // 2):
                    both = decode(code_from[a][h, q, :, lanes[some + n]])
                    both = both + BYTE * BYTE / 2
                    high = jnp.floor(both * (1.0 / BYTE))
                    codes[2 * n] = codes[2 * n] * BYTE + high
                    codes[2 * n + 1] = codes[2 * n + 1] * BYTE + (both - high * BYTE)
            for s in range(some):
                scale = scale_from[a, h, q, s * TILE : s * TILE + 1] * (1.0 / top_code)
                image[:, lanes[h * some + s]] += codes[s] * scale

        for h in range(HALVES):
            for distance in sorted({1, rows - 1}):
                arrive(h, distance)
            for g in range(groups):
                far_picked[h, g] = jnp.dot(
                    far_pick[g],
                    everything[h].reshape(rows * blocks, part_width),
                    preferred_element_type=jnp.float32,
                ).astype(jnp.bfloat16)

            for t in range(1, pairs + 1, 2):
                chosen = [lax.rem(chip + n, pairs) for n in (t, t + 1)]
                found = far(
                    [2 * q + 1 - core for q in chosen] + [2 * q + core for q in chosen],
                    far_picked=far_picked.at[h],
                )
                for n, q in enumerate(chosen):
                    to_partner[h, q] = found[n]
                    pair_copy(h, t + n - 1, q).start()
                    to_chips[h, q] = found[2 + n]

                @pl.loop(t - 2 if t > 1 else 1, t if t < pairs - 1 else pairs + 1)
                def _(i, h=h):
                    q = lax.rem(chip + i, pairs)
                    pair_copy(h, i - 1, q).wait_recv()
                    to_chips[h, q] = to_chips[h, q] + from_partner[h, q]

                    @pl.when(i < pairs)
                    def _():
                        pack(h, q)
                        for copy in chip_copies(h, i - 1, q, chip):
                            copy.start()

            if h == 0:
                between()
            if h == HALVES - 1:

                @pl.loop(0, near_groups)
                def _(g):
                    near(g)

        for h in range(HALVES):
            image[:, parts_of[h]] += to_chips[h, chip]
            for i in range(1, pairs):
                source = lax.rem(chip + pairs - i, pairs)
                for copy in chip_copies(h, i - 1, source, source):
                    copy.wait_recv()
                unpack(h, source)
        for h in range(HALVES):
            for distance in range(1, rows):
                each_hop(h, distance, lambda copy: copy.wait_send())
            for i in range(1, pairs + 1):
                q = lax.rem(chip + i, pairs)
                pair_copy(h, i - 1, q).wait_send()
                if i < pairs:
                    for copy in chip_copies(h, i - 1, q, chip):
                        copy.wait_send()

    basis_or_first = (first_ref, basis)

    def slot_codes(value, scales, buffer):
        for s in range(0, sides, 2):
            codes = []
            for side in (s, s + 1):
                code = to_code(value[:, lanes[side]], scales[side], TOP)
                codes.append(split_dot(to_mesh, code, 2).reshape(count, capacity, LANES))
            both = jnp.concatenate(codes, axis=1)
            buffer[:, s * capacity : (s + 2) * capacity, :] = narrow(both)

    to_own = one_hot(
        turned_target[:, 0:1] * capacity + rank_column == iota((blocks, slots), 1)
    )
    to_source = one_hot(turned_target[:, 0:1] == iota((blocks, count), 1))

    def home(buffer, scales):
        values = []
        own_scales = split_dot(to_source, scales)
        for s in range(0, sides, 2):
            both = decode(buffer[:, s * capacity : (s + 2) * capacity, :])
            for side in (s, s + 1):
                code = both[:, (side - s) * capacity : (side - s + 1) * capacity]
                code = code.reshape(slots, LANES)
                high = code.astype(jnp.bfloat16)
                scale = own_scales[:, side : side + 1] * (1.0 / TOP)
                values.append(
                    (
                        split_dot(to_own, high, 1) * scale,
                        split_dot(to_own, code - high.astype(jnp.float32), 1) * scale,
                    )
                )
        return values

    operate(0, lambda: None, lambda: None)
    found = [[] for _ in range(7)]
    for s in range(sides):
        one, two = first_ref[:, lanes[s]], image[:, lanes[s]]
        along, size = total_of(one * two), total_of(one * one)
        guess = jnp.where(size > 1e-30, along / jnp.maximum(size, 1e-30), 0.0)
        rest = two - guess * one
        for place, value in enumerate(
            (
                along,
                guess,
                total_of(one * rest),
                total_of(rest * rest),
                size,
                largest(two),
                largest(one),
            )
        ):
            found[place].append(value)
    table = share(0, [value for values in found for value in values])()
    total = jnp.sum(table, axis=0, keepdims=True)
    projects, seconds, basis_scale = [], [], jnp.zeros((count, LANES), jnp.float32)
    for s in range(sides):
        guess, cross, rest, size, top_image, top_first = [
            table[:, n * sides + s : n * sides + s + 1] for n in range(1, 7)
        ]
        project = single(total, s) / panels
        off = guess - project
        norm = jnp.sqrt(
            jnp.sum(rest + off * (2.0 * cross + off * size), axis=0, keepdims=True) / panels
            + epsilon
        )
        value = (image[:, lanes[s]] - project * first_ref[:, lanes[s]]) / norm
        basis[:, lanes[s]] = value
        own[s // some, :, lanes[s % some]] = value.astype(jnp.bfloat16)
        bound = (top_image + jnp.abs(project) * top_first) / norm
        basis_scale = basis_scale + jnp.where(iota((count, LANES), 1) == s, bound, 0.0)
        projects.append(project)
        seconds.append(norm)
    mine_scale = jnp.sum(
        jnp.where(iota((count, LANES), 0) == me, basis_scale, 0.0), axis=0, keepdims=True
    )
    every = pl.ds(0, sides * capacity)
    basis_start, basis_recv, basis_send = to_all(1, sent_basis, landed_basis, every)
    image_start, image_recv, image_send = to_all(2, sent_image, landed_image, every)

    def code_basis():
        slot_codes(basis[...], [single(mine_scale, s) for s in range(sides)], sent_basis)

    operate(1, code_basis, basis_start)
    scales = [largest(image[:, lanes[s]]) for s in range(sides)]
    slot_codes(image[...], scales, sent_image)
    image_start()
    values = []
    for source in (first_ref, basis):
        for s in range(sides):
            values.append(total_of(source[:, lanes[s]] * image[:, lanes[s]]))
    wait = share(1, values + scales)
    basis_recv()
    returned = home(landed_basis, basis_scale)
    for s in range(sides):
        basis_ref[stride[s], :], basis_rest_ref[stride[s], :] = returned[s]
    table = wait()
    total = jnp.sum(table, axis=0, keepdims=True) / panels
    ends = [[single(total, n * sides + s) for s in range(sides)] for n in range(2)]
    for s in range(sides):
        line = jnp.zeros((1, LANES), jnp.float32)
        for place, found in enumerate((norms, projects, seconds, ends[0], ends[1])):
            line = line + jnp.where(lane_row == place, found[s], 0.0)
        entries_ref[s : s + 1] = line[:, : entries_ref.shape[1]]
    kept = iota((count, LANES), 1)
    image_scale = jnp.zeros((count, LANES), jnp.float32)
    for s in range(sides):
        image_scale = image_scale + jnp.where(
            kept == s, table[:, 2 * sides + s : 2 * sides + s + 1], 0.0
        )
    image_recv()
    landed_values = home(landed_image, image_scale)
    for s in range(sides):
        high, rest = landed_values[s]
        next_ref[stride[s], :] = high + rest - ends[0][s] * (side_ref[stride[s], :] / norms[s])
        next_rest_ref[stride[s], :] = ends[1][s] * (returned[s][0] + returned[s][1])
    basis_send()
    image_send()


def body(
    right_side,
    cluster_of,
    near_rows,
    near_columns,
    near_blocks,
    far_rows,
    far_columns,
    far_rank,
    far_left,
    far_right,
):
    rows = lax.axis_size("row")
    columns = lax.axis_size("col")
    count = rows * columns
    blocks, sides, lanes = right_side.shape
    width = sides * lanes
    capacity = max(TILE, 2 * blocks // count)
    near_groups = near_rows.shape[0] // lanes
    near_blocks = near_blocks.reshape(near_groups, -1, *near_blocks.shape[1:])
    far_left = far_left.reshape(columns, -1, *far_left.shape[1:])
    far_right = far_right.reshape(columns, -1, *far_right.shape[1:])
    near_count, far_count = near_blocks.shape[1], far_left.shape[1]
    halo = blocks // 4
    pairs = columns // 2
    part = width // HALVES
    dma = pltpu.SemaphoreType.DMA
    real, half, code = jnp.float32, jnp.bfloat16, jnp.int16
    out_slots = (count, sides * capacity + TILE, lanes)
    code_slots = (count, sides * capacity, lanes)
    hbm = pl.BlockSpec(memory_space=pl.ANY)
    basis, basis_rest, following, following_rest, entries = pl.pallas_call(
        functools.partial(arnoldi_kernel, rows, columns),
        out_shape=[
            *[jax.ShapeDtypeStruct((blocks * sides, lanes), real)] * 4,
            jax.ShapeDtypeStruct((sides, 5), real),
        ],
        in_specs=[VMEM] * 7 + [hbm] * 3,
        out_specs=[VMEM] * 5,
        scratch_shapes=[
            pltpu.VMEM((near_groups + columns, TILE, lanes), real),
            pltpu.VMEM((near_groups, near_count, blocks + 2 * halo), half),
            pltpu.VMEM((near_groups, blocks, near_count), half),
            pltpu.VMEM((near_groups, near_count, width), real),
            pltpu.VMEM((columns, far_count, rows * blocks), half),
            pltpu.VMEM((columns, blocks, far_count), half),
            pltpu.VMEM((columns, far_count, lanes), real),
            pltpu.VMEM((HALVES, columns, far_count, part), half),
            pltpu.VMEM(out_slots, real),
            pltpu.VMEM(out_slots, real),
            pltpu.VMEM(code_slots, code),
            pltpu.VMEM(code_slots, code),
            pltpu.VMEM(code_slots, code),
            pltpu.VMEM(code_slots, code),
            pltpu.VMEM((blocks, width), real),
            pltpu.VMEM(near_blocks.shape, half),
            pltpu.VMEM(far_left.shape, half),
            pltpu.VMEM(far_right.shape, half),
            pltpu.VMEM((HALVES, blocks, part), half),
            pltpu.VMEM((blocks, width), real),
            pltpu.VMEM((blocks, width), real),
            pltpu.VMEM((HALVES, rows, blocks, part), half),
            pltpu.VMEM((blocks + 2 * halo, width), half),
            pltpu.VMEM((HALVES, halo, part), half),
            pltpu.VMEM((HALVES, halo, part), half),
            pltpu.VMEM((near_count, width), real),
            pltpu.VMEM((4, far_count, part), real),
            pltpu.VMEM((HALVES, pairs, blocks, part), real),
            pltpu.VMEM((HALVES, pairs, blocks, part), real),
            pltpu.VMEM((HALVES, pairs, blocks, part), real),
            pltpu.VMEM((HALVES, pairs, blocks, 3 * part // 2), code),
            pltpu.VMEM((HALVES, pairs, blocks, 3 * part // 2), code),
            pltpu.VMEM((HALVES, pairs, blocks, part), code),
            pltpu.VMEM((HALVES, pairs, blocks, part), code),
            pltpu.VMEM((2, HALVES, pairs, sides // HALVES * TILE, lanes), real),
            pltpu.VMEM((2, HALVES, pairs, sides // HALVES * TILE, lanes), real),
            pltpu.VMEM((2, TILE, lanes), real),
            pltpu.VMEM((2, count, TILE, lanes), real),
            dma((3, max(columns, near_groups))),
            dma((2, 2)),
            dma((2, 2)),
            dma((2, HALVES, 2, rows - 1)),
            dma((2, HALVES, 2, rows - 1)),
            dma((2, HALVES, pairs)),
            dma((2, HALVES, pairs)),
            dma((2, HALVES, pairs)),
            dma((2, HALVES, pairs)),
            dma((2, HALVES, pairs)),
            dma((2, HALVES, pairs)),
            dma((5,)),
            dma((5,)),
        ],
        compiler_params=pltpu.CompilerParams(
            collective_id=0, has_side_effects=True, vmem_limit_bytes=LIMIT
        ),
    )(
        right_side.reshape(blocks * sides, lanes),
        cluster_of.reshape(1, blocks),
        near_columns.reshape(near_groups, -1),
        near_rows.reshape(near_groups, -1),
        far_columns.reshape(columns, -1),
        far_rows.reshape(columns, -1),
        far_rank.reshape(columns, -1),
        near_blocks,
        far_left,
        far_right,
    )
    shape = (blocks, sides, lanes)
    return (
        (basis + basis_rest).reshape(shape),
        (following - following_rest).reshape(shape),
        entries.T,
    )


def solution(mesh):
    vector = P(("row", "col"), None, None)
    table = P(("row", "col"))
    placed = (vector, table, table, table, vector, table, table, table, vector, vector)
    return jax.shard_map(
        body,
        mesh=mesh,
        in_specs=placed,
        out_specs=(vector, vector, P()),
        check_vma=False,
    )
```
